256 devices in a mesh: item: 64 (over z, x, core), user: 4 (over y).
Axes of the slice: x: 4, y: 4, z: 8, core: 2. Of those that a mesh axis runs over, the one named last changes fastest.
Arguments:
- basis: float32 [32768, 128], P('item'), may hold values from -8 to 8
- old_values: float32 [128], replicated, may hold values from 0.5 to 2
- ratings: bfloat16 [256, 64, 128], P(('item', 'user')), may hold values from -16 to 16
- block_ids: int32 [256, 64], replicated, may hold values from 0 to 255, as said below
- user_row: int32 [256], replicated, may hold values from 0 to 255, as said below
Outputs:
- new_basis: float32 [32768, 128], P('item')
- user_factors: float32 [256, 128], replicated
The draws below stay inside these ranges and needn't reach their ends.
Inputs may be any that keep to these rules, and one draw needn't show every extreme that they name: `block_ids`: block g holds items g * 128 to g * 128 + 127; the 64 blocks of one user are distinct; at most 4 of one user's blocks lie in one slab of 512 items (items i * 512 to (i + 1) * 512 - 1), and every user has exactly 4 in some slab. A permutation: user j's tiles are row user_row[j] of ratings.
All inputs are finite; a program needn't handle non-finite values.
Results may differ from the reference program's by a relative error of at most 0.0003.
Values may be sent and summed in bfloat16 or wider, within the bound.
No kernel may reach another device: no remote copies, remote signals or barrier semaphores. Data moves between devices by JAX's collectives and lax.ppermute only.
A program may use at most 128 MiB of HBM per device.

```python
import math
import jax
import jax.numpy as jnp
from jax import lax

K = 128
USERS = 256
TILE = 128
ITEM_DEV = 512
CAP = 4
ITERS_CORE = 4
ITEMS = 32768
NBU = 64


def make_basis(key):
    subkeys = jax.random.split(jax.random.fold_in(key, 101), 4)
    noise = jnp.clip(jax.random.normal(subkeys[0], (ITEMS, K), jnp.float32), -4.0, 4.0)
    shared = jnp.clip(jax.random.normal(subkeys[1], (ITEMS, 1), jnp.float32), -4.0, 4.0)
    row_scale = jnp.exp(jax.random.uniform(subkeys[2], (ITEMS, 1), jnp.float32, math.log(0.5), math.log(2.0)))
    column_scale = jnp.exp(jax.random.uniform(subkeys[3], (1, K), jnp.float32, math.log(0.5), math.log(2.0)))
    return jnp.clip(row_scale * column_scale * (noise + 0.7 * shared), -8.0, 8.0)


def make_blocks(key):
    slabs = ITEMS // ITEM_DEV
    per_slab = ITEM_DEV // TILE
    anchor = jax.random.fold_in(key, 202)
    relabel = jax.random.permutation(jax.random.fold_in(anchor, 1), slabs)
    subkeys = jax.random.split(jax.random.fold_in(anchor, 2), USERS)

    def one_user(subkey):
        parts = jax.random.split(subkey, 6)
        first_draw = jax.random.randint(parts[0], (), 0, slabs)
        second_draw = jax.random.randint(parts[1], (), 0, slabs)
        heavy = relabel[first_draw * second_draw // slabs]
        others = (heavy + 1 + jax.random.permutation(parts[2], slabs - 1)[:NBU - CAP]) % slabs
        owners = jnp.concatenate([jnp.full((CAP,), heavy, dtype=jnp.int32), others.astype(jnp.int32)])
        places = jnp.concatenate([jax.random.permutation(parts[3], per_slab)[:CAP].astype(jnp.int32), jax.random.randint(parts[4], (NBU - CAP,), 0, per_slab)])
        chosen = owners * per_slab + places
        return chosen[jax.random.permutation(parts[5], NBU)]
    return jax.vmap(one_user)(subkeys).astype(jnp.int32)


def make_rows(key):
    return jax.random.permutation(jax.random.fold_in(key, 303), USERS).astype(jnp.int32)


def draw_basis(key, part):
    return make_basis(key)


def draw_block_ids(key, part):
    return make_blocks(key)


def draw_user_row(key, part):
    return make_rows(key)


def draw_ratings(key, part):
    basis = make_basis(key)
    chosen = make_blocks(key)
    placed = make_rows(key)
    inverse = jnp.zeros((USERS,), jnp.int32).at[placed].set(jnp.arange(USERS, dtype=jnp.int32))
    factor_column = jax.random.randint(jax.random.fold_in(key, 404), (USERS,), 0, K)
    positions = chosen[:, :, None] * TILE + jnp.arange(TILE, dtype=jnp.int32)[None, None, :]
    signal = basis[positions, factor_column[:, None, None]]
    noise = jnp.clip(jax.random.normal(jax.random.fold_in(key, 505), (USERS, NBU, TILE), jnp.float32), -4.0, 4.0)
    by_user = jnp.clip(1.5 * (noise + 2.0 * signal), -16.0, 16.0)
    return by_user[inverse].astype(jnp.bfloat16)


def setup_inputs(seed: int = 0) -> dict:
    key_of = jax.random.split(jax.random.key(seed), 6)
    basis = draw_basis(jax.random.fold_in(key_of[5], 71), 0)
    old_values = jnp.clip(jnp.exp(jax.random.uniform(key_of[1], (K,), jnp.float32, math.log(0.5), math.log(2.0))), 0.5, 2.0)
    ratings = draw_ratings(jax.random.fold_in(key_of[5], 71), 0)
    block_ids = draw_block_ids(jax.random.fold_in(key_of[5], 71), 0)
    user_row = draw_user_row(jax.random.fold_in(key_of[5], 71), 0)
    return dict(basis=basis, old_values=old_values, ratings=ratings, block_ids=block_ids, user_row=user_row)


exact_mode = lax.Precision.HIGHEST

def chol_lower(matrix):
    return jnp.linalg.cholesky(matrix)

def tri_inverse(lower_factor):
    order = lower_factor.shape[0]
    identity = jnp.eye(order, dtype=lower_factor.dtype)
    return lax.linalg.triangular_solve(lower_factor, identity, left_side=True, lower=True)

def orthonormalize(matrix):
    for turn in range(2):
        inner = jnp.dot(matrix.T, matrix, precision=exact_mode)
        inverse = tri_inverse(chol_lower(inner))
        matrix = jnp.dot(matrix, inverse.T, precision=exact_mode)
    return matrix

def core(chol_basis, old_values, projection, chol_first):
    basis_rank = chol_basis.shape[0]
    users = projection.shape[1]
    triangle = chol_first.T
    upper = jnp.concatenate([chol_basis.T * old_values[None, :], projection], axis=1)
    bottom = jnp.concatenate([jnp.zeros((users, basis_rank), chol_basis.dtype), triangle], axis=1)
    core_matrix = jnp.concatenate([upper, bottom], axis=0)
    core_gram = jnp.dot(core_matrix, core_matrix.T, precision=exact_mode)
    directions = jnp.eye(basis_rank + users, basis_rank, dtype=chol_basis.dtype)
    for sweep in range(ITERS_CORE):
        directions = orthonormalize(jnp.dot(core_gram, directions, precision=exact_mode))
    user_factors = jnp.dot(core_matrix[:, basis_rank:].T, directions, precision=exact_mode)
    return (directions, user_factors)

def reference(basis, old_values, ratings, block_ids, user_row):
    items = basis.shape[0]
    blocks = items // TILE
    by_user = ratings[user_row].astype(jnp.float32)
    slab = jnp.zeros((blocks, USERS, TILE), jnp.float32)
    slab = slab.at[block_ids, jnp.arange(USERS, dtype=jnp.int32)[:, None]].set(by_user)
    basis_tiles = basis.reshape(blocks, TILE, K)
    basis_gram = jnp.einsum('bik,bil->kl', basis_tiles, basis_tiles, precision=exact_mode) / items
    raw_proj = jnp.einsum('bik,bui->ku', basis_tiles, slab, precision=exact_mode)
    chol_basis = chol_lower(basis_gram)
    basis_inverse = tri_inverse(chol_basis)
    projection = jnp.dot(basis_inverse, raw_proj / items, precision=exact_mode)
    coefficients = jnp.dot(basis_inverse.T, projection, precision=exact_mode)
    residual = slab - jnp.einsum('bik,ku->bui', basis_tiles, coefficients, precision=exact_mode)
    first_gram = jnp.einsum('bui,bvi->uv', residual, residual, precision=exact_mode) / items
    chol_first = chol_lower(first_gram)
    first_orth = jnp.einsum('bvi,uv->bui', residual, tri_inverse(chol_first), precision=exact_mode)
    directions, user_factors = core(chol_basis, old_values, projection, chol_first)
    left_part = jnp.dot(basis_inverse.T, directions[:K], precision=exact_mode)
    rotated = jnp.einsum('bik,kj->bij', basis_tiles, left_part, precision=exact_mode)
    rotated = rotated + jnp.einsum('bui,uj->bij', first_orth, directions[K:], precision=exact_mode)
    return (rotated.reshape(items, K), user_factors)
```

```python
import functools

import jax
import jax.numpy as jnp
from jax import lax
from jax.experimental import pallas as pl
from jax.experimental.pallas import tpu as pltpu
from jax.sharding import Mesh
from jax.sharding import PartitionSpec as P

ITEM = ("item_0", "item_1", "item_2")
ITEM_USER = ("item_0", "item_1", "item_2", "user")

f32 = jnp.float32
exact_mode = lax.Precision.HIGHEST
RANK, USERS, ORDER = 128, 256, 384


def mm(a, b):
    return jnp.dot(a, b, precision=exact_mode, preferred_element_type=f32)


def mm_nt(a, b):
    return lax.dot_general(a, b, (((1,), (1,)), ((), ())), precision=exact_mode, preferred_element_type=f32)


def spread(x):
    return jnp.broadcast_to(x, (8, RANK))


def eliminate(gram):
    lane = lax.broadcasted_iota(jnp.int32, (8, RANK), 1)
    sub = lax.broadcasted_iota(jnp.int32, (8, RANK), 0)
    count = RANK // 8
    rows = [gram[8 * k : 8 * k + 8, :] for k in range(count)]
    pivots = []
    for panel in range(count):
        here = rows[panel]
        first = 8 * panel
        column = [spread(here[:, first + k : first + k + 1]) for k in range(8)]
        pivot_of_row = jnp.ones((8, RANK), f32)
        kept, inverses, uppers = [], [], []
        for s in range(8):
            upper = [spread(column[k][s : s + 1, :]) for k in range(s, 8)]
            inverse = 1.0 / upper[0]
            line = spread(here[s : s + 1, :])
            pivot_of_row = jnp.where(sub == s, upper[0], pivot_of_row)
            line = jnp.where(lane == first + s, line + line, line)
            kept.append(line)
            inverses.append(inverse)
            uppers.append(upper)
            factor = jnp.where(sub > s, column[s] * inverse, 0.0)
            here = here - factor * line
            for k in range(s + 1, 8):
                column[k] = column[k] - factor * upper[k - s]
        rows[panel] = here
        pivots.append(pivot_of_row)
        for other in range(panel + 1, count):
            there = rows[other]
            column = [spread(there[:, first + k : first + k + 1]) for k in range(8)]
            for s in range(8):
                factor = column[s] * inverses[s]
                there = there - factor * kept[s]
                for k in range(s + 1, 8):
                    column[k] = column[k] - factor * uppers[s][k - s]
            rows[other] = there
    return lower_of(jnp.concatenate(rows, axis=0)), jnp.concatenate(pivots, axis=0)


def square_iotas():
    i = lax.broadcasted_iota(jnp.int32, (RANK, RANK), 0)
    k = lax.broadcasted_iota(jnp.int32, (RANK, RANK), 1)
    return i, k


def lower_of(x):
    i, k = square_iotas()
    return jnp.where(i >= k, x, 0.0)


def eliminate_slowly(gram):
    i, k = square_iotas()

    def step(j, carry):
        x, pivots = carry
        line = jnp.sum(jnp.where(i == j, x, 0.0), axis=0, keepdims=True)
        column = jnp.sum(jnp.where(k == j, x, 0.0), axis=1, keepdims=True)
        pivot = jnp.sum(jnp.where((i == j) & (k == j), x, 0.0), axis=(0, 1), keepdims=True)
        pivots = jnp.where(i == j, pivot, pivots)
        doubled = jnp.where(k[:1] == j, line + line, line)
        x = x - jnp.where(i > j, column / pivot, 0.0) * doubled
        return x, pivots

    x, pivots = lax.fori_loop(0, RANK, step, (gram, jnp.ones((RANK, RANK), f32)))
    return lower_of(x), pivots


def scaled(x, pivots, power):
    factor = 1.0 / pivots if power == 1 else lax.rsqrt(pivots)
    return jnp.concatenate([x[:, c : c + RANK] * factor for c in range(0, x.shape[1], RANK)], axis=1)


def turned(lower, pivots, x):
    return scaled(mm(lower, scaled(x, pivots, 1)), pivots, 2)


def smallest(pivots, gram):
    i, k = square_iotas()
    start = jnp.sum(jnp.where(i == k, gram, 0.0), axis=1, keepdims=True)
    return jnp.min(pivots / start)


def polished(x, y):
    i, k = square_iotas()
    off = mm_nt(x, y) - jnp.where(i == k, 1.0, 0.0)
    step = jnp.where(i > k, off, jnp.where(i == k, 0.5 * off, 0.0))
    return x - mm(step, x), y - mm(step, y)


def assemble(sums, weights, items):
    i, k = square_iotas()
    block = lambda n: sums[RANK * n : RANK * (n + 1), :] * (1.0 / items)
    own = jnp.transpose(block(0) * weights) * weights
    left1, left2 = block(1) * weights, block(2) * weights
    c11, c12, c22 = block(3), block(4), block(5)
    diagonal = jnp.where(i == k, own + c11 + c22, 0.0)
    size = jnp.sum(diagonal, axis=(0, 1), keepdims=True)
    whole = jnp.concatenate(
        [
            jnp.concatenate([own, jnp.transpose(left1), jnp.transpose(left2)], axis=1),
            jnp.concatenate([left1, c11, c12], axis=1),
            jnp.concatenate([left2, jnp.transpose(c12), c22], axis=1),
        ],
        axis=0,
    )
    return whole * (1.0 / size), size


def core_kernel(items, sums_ref, weights_ref, turn_ref, left_ref, factors_ref, gram_ref, turn_t_ref, back_ref):
    weights = weights_ref[...]
    whole, size = assemble(sums_ref, weights, items)
    gram_ref[...] = whole
    g = gram_ref[...]

    x = g[:RANK, :]
    h1 = mm_nt(x, x)
    low1, piv1 = eliminate(h1)
    x = turned(low1, piv1, x)
    x = mm(x, g)
    y = mm(x, g)
    h2 = mm_nt(x, y)
    low2, piv2 = eliminate(h2)
    x = turned(low2, piv2, y)
    x = mm(x, g)
    y = mm(x, g)
    h3 = mm_nt(x, y)
    low3, piv3 = eliminate(h3)
    turn_t_ref[...] = turned(low3, piv3, x)
    back_ref[...] = turned(low3, piv3, y)
    fine = (smallest(piv1, h1) > 1e-4) & (smallest(piv2, h2) > 3e-4) & (smallest(piv3, h3) > 8e-3)

    @pl.when(jnp.logical_not(fine))
    def _():
        def ortho(x, y):
            gram = mm_nt(x, y)
            return eliminate_slowly(gram)

        def sweep(n, x):
            y = mm(x, gram_ref[...])
            low, piv = ortho(x, y)
            y = turned(low, piv, y)
            low, piv = ortho(y, y)
            return turned(low, piv, y)

        start = jnp.where(
            lax.broadcasted_iota(jnp.int32, (RANK, ORDER), 0) == lax.broadcasted_iota(jnp.int32, (RANK, ORDER), 1), 1.0, 0.0
        )
        x = lax.fori_loop(0, 4, sweep, start)
        y = mm(x, gram_ref[...])
        low, piv = ortho(x, y)
        x, y = turned(low, piv, x), turned(low, piv, y)
        x, y = polished(x, y)
        x, y = polished(x, y)
        turn_t_ref[...] = x
        back_ref[...] = y

    scale = lax.rsqrt(size)
    x = turn_t_ref[...] * scale
    left_ref[:, :RANK] = x[:, :RANK] * weights
    left_ref[:, RANK:] = x[:, RANK:]
    user_of = turn_ref[...]
    onehot = jnp.where(lax.broadcasted_iota(jnp.int32, (USERS, USERS), 1) == user_of, 1.0, 0.0)
    factors_ref[...] = mm_nt(onehot, back_ref[:, RANK:] * (scale * size))


def core(sums, weights, user_row, items):
    return pl.pallas_call(
        functools.partial(core_kernel, items),
        out_shape=[jax.ShapeDtypeStruct((RANK, ORDER), f32), jax.ShapeDtypeStruct((USERS, RANK), f32)],
        scratch_shapes=[pltpu.VMEM((ORDER, ORDER), f32), pltpu.VMEM((RANK, ORDER), f32), pltpu.VMEM((RANK, ORDER), f32)],
        compiler_params=pltpu.CompilerParams(vmem_limit_bytes=32 * 2**20),
    )(sums, weights.reshape(1, RANK), user_row.reshape(USERS, 1))


def column_kernel(row_ref, user_row_ref, blocks_ref, tiles_ref, out_ref):
    mine = user_row_ref[...] == row_ref[0]
    blocks = jnp.sum(jnp.where(mine, blocks_ref[...], 0), axis=1, keepdims=True)
    count = out_ref.shape[0]
    place = lax.broadcasted_iota(jnp.int32, (blocks.shape[0], count), 1) == blocks
    place = jnp.where(place, 1.0, 0.0).astype(jnp.bfloat16)
    dense = lax.dot_general(place, tiles_ref[...], (((0,), (0,)), ((), ())), preferred_element_type=f32)
    out_ref[...] = dense.astype(jnp.bfloat16)


def column_of(row, user_row, block_ids, tiles, count):
    in_vmem = pl.BlockSpec(memory_space=pltpu.VMEM)
    return pl.pallas_call(
        column_kernel,
        out_shape=jax.ShapeDtypeStruct((count, tiles.shape[1]), jnp.bfloat16),
        in_specs=[pl.BlockSpec(memory_space=pltpu.SMEM), in_vmem, in_vmem, in_vmem],
        out_specs=in_vmem,
    )(row.reshape(1), user_row.reshape(1, -1), block_ids.T, tiles)


def gram_kernel(basis_ref, slab_ref, out_ref):
    width = slab_ref.shape[2]
    own = left = cross = 0.0
    for b in range(slab_ref.shape[0]):
        rows = basis_ref[width * b : width * (b + 1), :]
        x = slab_ref[b]
        own = own + lax.dot_general(rows, rows, (((0,), (0,)), ((), ())), precision=exact_mode, preferred_element_type=f32)
        left = left + mm(x.astype(f32), rows)
        cross = cross + lax.dot_general(x, x, (((1,), (1,)), ((), ())), preferred_element_type=f32)
    out_ref[0:128, :] = own
    out_ref[128:384, :] = left
    out_ref[384:512, :] = cross[:128, :128]
    out_ref[512:640, :] = cross[:128, 128:]
    out_ref[640:768, :] = cross[128:, 128:]


def gram_parts(basis, slab):
    return pl.pallas_call(gram_kernel, out_shape=jax.ShapeDtypeStruct((768, RANK), f32))(basis, slab)


def rows_kernel(basis_ref, slab_ref, left_ref, out_ref):
    width = slab_ref.shape[2]
    for b in range(slab_ref.shape[0]):
        here = slice(width * b, width * (b + 1))
        x = jnp.transpose(slab_ref[b].astype(f32))
        out_ref[here, :] = mm_nt(basis_ref[here, :], left_ref[:, :RANK]) + mm_nt(x, left_ref[:, RANK:])


def new_rows(basis, slab, left):
    return pl.pallas_call(rows_kernel, out_shape=jax.ShapeDtypeStruct(basis.shape, f32))(basis, slab, left)


def copies(x, axis):
    x = jnp.broadcast_to(x, (lax.axis_size(axis), *x.shape))
    return lax.all_to_all(x, axis, split_axis=0, concat_axis=0, tiled=True)


def summed(parts):
    far = ("item_0", "item_1")
    pieces = parts.reshape(2, lax.axis_size(far), -1, RANK)
    near = lax.all_to_all(pieces, "item_2", 0, 0, tiled=True).sum(axis=0)
    own = lax.all_to_all(near, far, 0, 0, tiled=True).sum(axis=0)
    half = copies(own, far)
    return copies(half, "item_2").reshape(parts.shape)


def per_device(basis, old_values, ratings, block_ids, user_row):
    n_item = lax.axis_size(ITEM)
    n_user = lax.axis_size("user")
    width = ratings.shape[2]
    slab_blocks = basis.shape[0] // width
    row = lax.axis_index(ITEM) * n_user + lax.axis_index("user")
    column = column_of(row, user_row, block_ids, ratings[0], n_item * slab_blocks)
    arrived = lax.all_to_all(column.reshape(n_item, slab_blocks, width), ITEM, 0, 0, tiled=True)
    pooled = copies(arrived, "user")
    slab = pooled.reshape(USERS, slab_blocks, width).swapaxes(0, 1)
    sums = summed(gram_parts(basis, slab))
    place = user_row % n_user * n_item + user_row // n_user
    left, user_factors = core(sums, old_values, place, basis.shape[0] * n_item)
    return new_rows(basis, slab, left), user_factors


def solution(mesh):
    finer = Mesh(
        mesh.devices.reshape(8, 4, 2, mesh.shape["user"]), ("item_0", "item_1", "item_2", "user")
    )
    placed = (P(ITEM, None), P(), P(ITEM_USER, None, None), P(), P())
    return jax.shard_map(
        per_device, mesh=finer, in_specs=placed, out_specs=(P(ITEM, None), P()), check_vma=False
    )
```

```python
import functools

import jax
import jax.numpy as jnp
from jax import lax
from jax.experimental import pallas as pl
from jax.experimental.pallas import tpu as pltpu
from jax.sharding import Mesh
from jax.sharding import PartitionSpec as P

ITEM = ("item_0", "item_1", "item_2")
ITEM_USER = ("item_0", "item_1", "item_2", "user")

f32 = jnp.float32
exact_mode = lax.Precision.HIGHEST
RANK, USERS, ORDER, CAP = 128, 256, 384, 4


def split(x):
    high = x.astype(jnp.bfloat16)
    rest = x - high.astype(f32)
    middle = rest.astype(jnp.bfloat16)
    return high, middle, (rest - middle.astype(f32)).astype(jnp.bfloat16)


def product(a, b, dims):
    n = a[0].shape[0]
    one = lambda x, y: lax.dot_general(x, y, (dims, ((), ())), preferred_element_type=f32)
    p = one(jnp.concatenate(a, axis=0), b[0])
    q = one(jnp.concatenate(a[:2], axis=0), b[1])
    r = one(a[0], b[2])
    return p[:n] + ((p[n : 2 * n] + q[:n]) + ((p[2 * n :] + q[n:]) + r))


def mm(a, b):
    a = a if isinstance(a, tuple) else split(a)
    b = b if isinstance(b, tuple) else split(b)
    return product(a, b, ((1,), (0,)))


def mm_nt(a, b):
    a = a if isinstance(a, tuple) else split(a)
    b = b if isinstance(b, tuple) else split(b)
    return product(a, b, ((1,), (1,)))


def spread(x):
    return jnp.broadcast_to(x, (8, RANK))


def eliminate(gram):
    lane = lax.broadcasted_iota(jnp.int32, (8, RANK), 1)
    sub = lax.broadcasted_iota(jnp.int32, (8, RANK), 0)
    count = RANK // 8
    rows = [gram[8 * k : 8 * k + 8, :] for k in range(count)]
    pivots = []
    for panel in range(count):
        here = rows[panel]
        first = 8 * panel
        column = [spread(here[:, first + k : first + k + 1]) for k in range(8)]
        pivot_of_row = jnp.ones((8, RANK), f32)
        steps = []
        for s in range(0, 8, 2):
            upper = [spread(column[k][s : s + 1, :]) for k in range(s, 8)]
            under = [spread(column[k][s + 1 : s + 2, :]) for k in range(s + 1, 8)]
            a, b, c = upper[0], upper[1], under[0]
            det = a * c - b * b
            inverse = 1.0 / a
            second = 1.0 / det
            ratio = b * inverse
            line = spread(here[s : s + 1, :])
            line = jnp.where(lane == first + s, line + line, line)
            next_line = spread(here[s + 1 : s + 2, :]) - ratio * line
            next_line = jnp.where(lane == first + s + 1, next_line + next_line, next_line)
            pivot_of_row = jnp.where(sub == s, a, jnp.where(sub == s + 1, det * inverse, pivot_of_row))
            next_inverse, mixed = a * second, b * second
            under = [x - ratio * y for x, y in zip(under, upper[1:])]
            steps.append((inverse, line, upper))
            steps.append((next_inverse, next_line, under))
            one = jnp.where(sub > s, column[s] * inverse, 0.0)
            two = jnp.where(sub > s + 1, column[s + 1] * next_inverse - column[s] * mixed, 0.0)
            here = here - one * line - two * next_line
            for k in range(s + 2, 8):
                column[k] = column[k] - one * upper[k - s] - two * under[k - s - 1]
        rows[panel] = here
        pivots.append(pivot_of_row)
        for other in range(panel + 1, count):
            there = rows[other]
            column = [spread(there[:, first + k : first + k + 1]) for k in range(8)]
            for s, (inverse, line, upper) in enumerate(steps):
                factor = column[s] * inverse
                there = there - factor * line
                for k in range(s + 1, 8):
                    column[k] = column[k] - factor * upper[k - s]
            rows[other] = there
    return lower_of(jnp.concatenate(rows, axis=0)), jnp.concatenate(pivots, axis=0)


def square_iotas():
    i = lax.broadcasted_iota(jnp.int32, (RANK, RANK), 0)
    k = lax.broadcasted_iota(jnp.int32, (RANK, RANK), 1)
    return i, k


def lower_of(x):
    i, k = square_iotas()
    return jnp.where(i >= k, x, 0.0)


def eliminate_slowly(gram):
    i, k = square_iotas()

    def step(j, carry):
        x, pivots = carry
        line = jnp.sum(jnp.where(i == j, x, 0.0), axis=0, keepdims=True)
        column = jnp.sum(jnp.where(k == j, x, 0.0), axis=1, keepdims=True)
        pivot = jnp.sum(jnp.where((i == j) & (k == j), x, 0.0), axis=(0, 1), keepdims=True)
        pivots = jnp.where(i == j, pivot, pivots)
        doubled = jnp.where(k[:1] == j, line + line, line)
        x = x - jnp.where(i > j, column / pivot, 0.0) * doubled
        return x, pivots

    x, pivots = lax.fori_loop(0, RANK, step, (gram, jnp.ones((RANK, RANK), f32)))
    return lower_of(x), pivots


def scaled(x, pivots, power):
    factor = 1.0 / pivots if power == 1 else lax.rsqrt(pivots)
    return jnp.concatenate([x[:, c : c + RANK] * factor for c in range(0, x.shape[1], RANK)], axis=1)


def turned(lower, pivots, x):
    return scaled(mm(lower, scaled(x, pivots, 1)), pivots, 2)


def smallest(pivots, gram):
    i, k = square_iotas()
    start = jnp.sum(jnp.where(i == k, gram, 0.0), axis=1, keepdims=True)
    return jnp.min(pivots / start)


def polished(x, y):
    i, k = square_iotas()
    off = mm_nt(x, y) - jnp.where(i == k, 1.0, 0.0)
    step = jnp.where(i > k, off, jnp.where(i == k, 0.5 * off, 0.0))
    return x - mm(step, x), y - mm(step, y)


def assemble(sums, weights, items):
    i, k = square_iotas()
    block = lambda n: sums[RANK * n : RANK * (n + 1), :] * (1.0 / items)
    own = jnp.transpose(block(0) * weights) * weights
    left1, left2 = block(1) * weights, block(2) * weights
    c11, c12, c22 = block(3), block(4), block(5)
    diagonal = jnp.where(i == k, own + c11 + c22, 0.0)
    size = jnp.sum(diagonal, axis=(0, 1), keepdims=True)
    whole = jnp.concatenate(
        [
            jnp.concatenate([own, jnp.transpose(left1), jnp.transpose(left2)], axis=1),
            jnp.concatenate([left1, c11, c12], axis=1),
            jnp.concatenate([left2, jnp.transpose(c12), c22], axis=1),
        ],
        axis=0,
    )
    return whole * (1.0 / size), size


def core_kernel(
    items, at_ref, near_ref, far1_ref, far2_ref, far3_ref, wide_ref, weights_ref, place_ref,
    rows_ref, factors_ref, sums_ref, gram_ref, turn_t_ref, back_ref,
):
    half, ring = at_ref[0], at_ref[1]
    piece = near_ref.shape[1]
    for k, ref in enumerate((near_ref, far1_ref, far2_ref, far3_ref)):
        chunk = lax.rem(ring + 4 - k, 4)
        for j in range(2):
            first = ((half if j == 0 else 1 - half) * 4 + chunk) * piece
            sums_ref[pl.ds(pl.multiple_of(first, 8), piece), :] = ref[j]
    weights = weights_ref[...]
    whole, size = assemble(sums_ref, weights, items)
    gram_ref[...] = whole
    g = split(whole)

    x = whole[:RANK, :]
    first = tuple(part[:RANK, :] for part in g)
    h1 = mm_nt(first, first)
    low1, piv1 = eliminate(h1)
    x = turned(low1, piv1, x)
    x = mm(x, g)
    y = mm(x, g)
    h2 = mm_nt(x, y)
    low2, piv2 = eliminate(h2)
    x = turned(low2, piv2, y)
    x = mm(x, g)
    y = mm(x, g)
    h3 = mm_nt(x, y)
    low3, piv3 = eliminate(h3)
    turn_t_ref[...] = turned(low3, piv3, x)
    back_ref[...] = turned(low3, piv3, y)
    fine = (smallest(piv1, h1) > 1e-4) & (smallest(piv2, h2) > 3e-4) & (smallest(piv3, h3) > 8e-3)

    @pl.when(jnp.logical_not(fine))
    def _():
        def ortho(x, y):
            gram = mm_nt(x, y)
            return eliminate_slowly(gram)

        def sweep(n, x):
            y = mm(x, gram_ref[...])
            low, piv = ortho(x, y)
            y = turned(low, piv, y)
            low, piv = ortho(y, y)
            return turned(low, piv, y)

        start = jnp.where(
            lax.broadcasted_iota(jnp.int32, (RANK, ORDER), 0) == lax.broadcasted_iota(jnp.int32, (RANK, ORDER), 1), 1.0, 0.0
        )
        x = lax.fori_loop(0, 4, sweep, start)
        y = mm(x, gram_ref[...])
        low, piv = ortho(x, y)
        x, y = turned(low, piv, x), turned(low, piv, y)
        x, y = polished(x, y)
        x, y = polished(x, y)
        turn_t_ref[...] = x
        back_ref[...] = y

    scale = lax.rsqrt(size)
    x = turn_t_ref[...] * scale
    left = jnp.concatenate([x[:, :RANK] * weights, x[:, RANK:]], axis=1)
    rows_ref[...] = mm_nt(wide_ref[...], left)
    user_of = place_ref[...]
    onehot = jnp.where(lax.broadcasted_iota(jnp.int32, (USERS, USERS), 1) == user_of, 1.0, 0.0)
    factors_ref[...] = mm_nt(onehot, back_ref[:, RANK:] * (scale * size))


def core(at, pieces, wide, weights, place, items):
    in_vmem = pl.BlockSpec(memory_space=pltpu.VMEM)
    count, order = wide.shape
    return pl.pallas_call(
        functools.partial(core_kernel, items),
        out_shape=[jax.ShapeDtypeStruct((count, RANK), f32), jax.ShapeDtypeStruct((USERS, RANK), f32)],
        in_specs=[pl.BlockSpec(memory_space=pltpu.SMEM)] + [in_vmem] * 7,
        scratch_shapes=[
            pltpu.VMEM((2 * order, RANK), f32),
            pltpu.VMEM((order, order), f32),
            pltpu.VMEM((RANK, order), f32),
            pltpu.VMEM((RANK, order), f32),
        ],
        compiler_params=pltpu.CompilerParams(vmem_limit_bytes=32 * 2**20),
    )(at, *pieces, wide, weights.reshape(1, RANK), place.reshape(-1, 1))


def column_kernel(row_ref, user_row_ref, blocks_ref, tiles_ref, out_ref):
    mine = user_row_ref[...] == row_ref[0]
    blocks = jnp.sum(jnp.where(mine, blocks_ref[...], 0), axis=1, keepdims=True)
    count = out_ref.shape[0]
    place = lax.broadcasted_iota(jnp.int32, (blocks.shape[0], count), 1) == blocks
    place = jnp.where(place, 1.0, 0.0).astype(jnp.bfloat16)
    dense = lax.dot_general(place, tiles_ref[...], (((0,), (0,)), ((), ())), preferred_element_type=f32)
    out_ref[...] = dense.astype(jnp.bfloat16)


def column_of(row, user_row, block_ids, tiles, count):
    in_vmem = pl.BlockSpec(memory_space=pltpu.VMEM)
    return pl.pallas_call(
        column_kernel,
        out_shape=jax.ShapeDtypeStruct((count, tiles.shape[1]), jnp.bfloat16),
        in_specs=[pl.BlockSpec(memory_space=pltpu.SMEM), in_vmem, in_vmem, in_vmem],
        out_specs=in_vmem,
    )(row.reshape(1), user_row.reshape(1, -1), block_ids.T, tiles)


def strips(refs, flat_ref):
    pieces = []
    for ref in refs:
        flat_ref[...] = ref[...].astype(f32)
        count = flat_ref.shape[0] // CAP
        blocks = [flat_ref[pl.ds(b, count, stride=CAP), :] for b in range(CAP)]
        pieces.append(jnp.concatenate(blocks, axis=1))
    return jnp.concatenate(pieces, axis=0)


def gram_kernel(at_ref, basis_ref, x0_ref, x1_ref, x2_ref, x3_ref, keep_ref, send_ref, flat_ref):
    x = strips((x0_ref, x1_ref, x2_ref, x3_ref), flat_ref).astype(jnp.bfloat16)
    parts = split(basis_ref[...])
    high_t, middle_t = (jnp.transpose(p.astype(f32)).astype(jnp.bfloat16) for p in parts[:2])
    one = lambda a, b: jnp.dot(a, b, preferred_element_type=f32)
    both = one(jnp.concatenate([x, high_t], axis=0), jnp.concatenate(parts, axis=1))
    strip = lambda rows, k: both[rows, RANK * k : RANK * (k + 1)]
    users, rest = slice(0, USERS), slice(USERS, None)
    left = strip(users, 0) + (strip(users, 1) + strip(users, 2))
    small = strip(rest, 1) + strip(rest, 2)
    own = strip(rest, 0) + (small + jnp.transpose(small) + one(middle_t, parts[1]))
    cross = lax.dot_general(x, x, (((1,), (1,)), ((), ())), preferred_element_type=f32)
    low = [own, left[:RANK], left[RANK:]]
    high = [cross[:RANK, :RANK], cross[:RANK, RANK:], cross[RANK:, RANK:]]
    half = at_ref[0]
    for k in range(3):
        keep_ref[RANK * k : RANK * (k + 1), :] = jnp.where(half == 0, low[k], high[k])
        send_ref[RANK * k : RANK * (k + 1), :] = jnp.where(half == 0, high[k], low[k])


def gram_parts(at, basis, pieces):
    in_vmem = pl.BlockSpec(memory_space=pltpu.VMEM)
    return pl.pallas_call(
        gram_kernel,
        out_shape=[jax.ShapeDtypeStruct((3 * RANK, RANK), f32)] * 2,
        in_specs=[pl.BlockSpec(memory_space=pltpu.SMEM)] + [in_vmem] * 5,
        scratch_shapes=[pltpu.VMEM(pieces[0].shape, f32)],
        compiler_params=pltpu.CompilerParams(vmem_limit_bytes=32 * 2**20),
    )(at, basis, *pieces)


def wide_kernel(basis_ref, x0_ref, x1_ref, x2_ref, x3_ref, out_ref, flat_ref):
    out_ref[:, :RANK] = basis_ref[...]
    out_ref[:, RANK:] = jnp.transpose(strips((x0_ref, x1_ref, x2_ref, x3_ref), flat_ref))


def wide_of(basis, pieces):
    in_vmem = pl.BlockSpec(memory_space=pltpu.VMEM)
    return pl.pallas_call(
        wide_kernel,
        out_shape=jax.ShapeDtypeStruct((basis.shape[0], RANK + USERS), f32),
        in_specs=[in_vmem] * 5,
        scratch_shapes=[pltpu.VMEM(pieces[0].shape, f32)],
        compiler_params=pltpu.CompilerParams(vmem_limit_bytes=32 * 2**20),
    )(basis, *pieces)


def around(x, axis):
    n = lax.axis_size(axis)
    return [lax.ppermute(x, axis, [(i, (i + k) % n) for i in range(n)]) for k in range(1, n)]


def summed(keep, send):
    other = [(0, 1), (1, 0)]
    total = keep + lax.ppermute(send, "item_2", other)
    n = lax.axis_size("item_1")
    rows = total.shape[0] // n
    here = lax.axis_index("item_1")
    part = lambda k: lax.dynamic_slice_in_dim(total, (here + k) % n * rows, rows)
    own = part(0)
    for k in range(1, n):
        own = own + lax.ppermute(part(k), "item_1", [(i, (i + k) % n) for i in range(n)])
    far = lax.axis_size("item_0")
    every = lax.all_to_all(jnp.broadcast_to(own, (far, *own.shape)), "item_0", 0, 0, tiled=True)
    own = jnp.sum(every, axis=0)
    pair = jnp.stack([own, lax.ppermute(own, "item_2", other)])
    return [pair] + around(pair, "item_1")


def per_device(basis, old_values, ratings, block_ids, user_row):
    n_item = lax.axis_size(ITEM)
    n_user = lax.axis_size("user")
    width = ratings.shape[2]
    slab_blocks = basis.shape[0] // width
    row = lax.axis_index(ITEM) * n_user + lax.axis_index("user")
    column = column_of(row, user_row, block_ids, ratings[0], n_item * slab_blocks)
    arrived = lax.all_to_all(column.reshape(n_item, slab_blocks, width), ITEM, 0, 0, tiled=True)
    arrived = arrived.reshape(n_item * slab_blocks, width)
    pieces = [arrived] + around(arrived, "user")
    at = jnp.stack([lax.axis_index("item_2"), lax.axis_index("item_1")]).astype(jnp.int32)
    keep, send = gram_parts(at, basis, pieces)
    wide = wide_of(basis, pieces)
    sums = summed(keep, send)
    steps = (lax.axis_index("user") - user_row % n_user) % n_user
    place = steps * n_item + user_row // n_user
    return tuple(core(at, sums, wide, old_values, place, basis.shape[0] * n_item))


def solution(mesh):
    finer = Mesh(
        mesh.devices.reshape(8, 4, 2, mesh.shape["user"]), ("item_0", "item_1", "item_2", "user")
    )
    placed = (P(ITEM, None), P(), P(ITEM_USER, None, None), P(), P())
    return jax.shard_map(
        per_device, mesh=finer, in_specs=placed, out_specs=(P(ITEM, None), P()), check_vma=False
    )
```

```python
import functools

import jax
import jax.numpy as jnp
from jax import lax
from jax.experimental import pallas as pl
from jax.experimental.pallas import tpu as pltpu
from jax.sharding import Mesh
from jax.sharding import PartitionSpec as P

ITEM = ("item_0", "item_1", "item_2")
ITEM_USER = ("item_0", "item_1", "item_2", "user")

f32 = jnp.float32
RANK, USERS, ORDER, CAP = 128, 256, 384, 4


def split(x):
    high = x.astype(jnp.bfloat16)
    rest = x - high.astype(f32)
    middle = rest.astype(jnp.bfloat16)
    return high, middle, (rest - middle.astype(f32)).astype(jnp.bfloat16)


def product(a, b, dims):
    n = a[0].shape[0]
    one = lambda x, y: lax.dot_general(x, y, (dims, ((), ())), preferred_element_type=f32)
    p = one(jnp.concatenate(a, axis=0), b[0])
    q = one(jnp.concatenate(a[:2], axis=0), b[1])
    r = one(a[0], b[2])
    return p[:n] + ((p[n : 2 * n] + q[:n]) + ((p[2 * n :] + q[n:]) + r))


def mm(a, b):
    a = a if isinstance(a, tuple) else split(a)
    b = b if isinstance(b, tuple) else split(b)
    return product(a, b, ((1,), (0,)))


def mm_nt(a, b):
    a = a if isinstance(a, tuple) else split(a)
    b = b if isinstance(b, tuple) else split(b)
    return product(a, b, ((1,), (1,)))


def spread(x):
    return jnp.broadcast_to(x, (8, RANK))


def eliminate(gram):
    lane = lax.broadcasted_iota(jnp.int32, (8, RANK), 1)
    sub = lax.broadcasted_iota(jnp.int32, (8, RANK), 0)
    count = RANK // 8
    rows = [gram[8 * k : 8 * k + 8, :] for k in range(count)]
    pivots = []
    for panel in range(count):
        here = rows[panel]
        first = 8 * panel
        column = [spread(here[:, first + k : first + k + 1]) for k in range(8)]
        pivot_of_row = jnp.ones((8, RANK), f32)
        steps = []
        for s in range(0, 8, 2):
            upper = [spread(column[k][s : s + 1, :]) for k in range(s, 8)]
            under = [spread(column[k][s + 1 : s + 2, :]) for k in range(s + 1, 8)]
            a, b, c = upper[0], upper[1], under[0]
            det = a * c - b * b
            inverse = 1.0 / a
            second = 1.0 / det
            ratio = b * inverse
            line = spread(here[s : s + 1, :])
            line = jnp.where(lane == first + s, line + line, line)
            next_line = spread(here[s + 1 : s + 2, :]) - ratio * line
            next_line = jnp.where(lane == first + s + 1, next_line + next_line, next_line)
            pivot_of_row = jnp.where(sub == s, a, jnp.where(sub == s + 1, det * inverse, pivot_of_row))
            next_inverse, mixed = a * second, b * second
            under = [x - ratio * y for x, y in zip(under, upper[1:])]
            steps.append((inverse, line, upper))
            steps.append((next_inverse, next_line, under))
            one = jnp.where(sub > s, column[s] * inverse, 0.0)
            two = jnp.where(sub > s + 1, column[s + 1] * next_inverse - column[s] * mixed, 0.0)
            here = here - one * line - two * next_line
            for k in range(s + 2, 8):
                column[k] = column[k] - one * upper[k - s] - two * under[k - s - 1]
        rows[panel] = here
        pivots.append(pivot_of_row)
        for other in range(panel + 1, count):
            there = rows[other]
            column = [spread(there[:, first + k : first + k + 1]) for k in range(8)]
            for s, (inverse, line, upper) in enumerate(steps):
                factor = column[s] * inverse
                there = there - factor * line
                for k in range(s + 1, 8):
                    column[k] = column[k] - factor * upper[k - s]
            rows[other] = there
    return lower_of(jnp.concatenate(rows, axis=0)), jnp.concatenate(pivots, axis=0)


def square_iotas():
    i = lax.broadcasted_iota(jnp.int32, (RANK, RANK), 0)
    k = lax.broadcasted_iota(jnp.int32, (RANK, RANK), 1)
    return i, k


def lower_of(x):
    i, k = square_iotas()
    return jnp.where(i >= k, x, 0.0)


def scaled(x, pivots, power):
    factor = 1.0 / pivots if power == 1 else lax.rsqrt(pivots)
    return jnp.concatenate([x[:, c : c + RANK] * factor for c in range(0, x.shape[1], RANK)], axis=1)


def turned(lower, pivots, x):
    return scaled(mm(lower, scaled(x, pivots, 1)), pivots, 2)


def smallest(pivots, gram):
    i, k = square_iotas()
    start = jnp.sum(jnp.where(i == k, gram, 0.0), axis=1, keepdims=True)
    return jnp.min(pivots / start)


def polished(x, y):
    i, k = square_iotas()
    off = mm_nt(x, y) - jnp.where(i == k, 1.0, 0.0)
    step = jnp.where(i > k, off, jnp.where(i == k, 0.5 * off, 0.0))
    return x - mm(step, x), y - mm(step, y)


def assemble(sums, weights, items):
    i, k = square_iotas()
    block = lambda n: sums[RANK * n : RANK * (n + 1), :] * (1.0 / items)
    own = jnp.transpose(block(0) * weights) * weights
    left1, left2 = block(1) * weights, block(2) * weights
    c11, c12, c22 = block(3), block(4), block(5)
    diagonal = jnp.where(i == k, own + c11 + c22, 0.0)
    size = jnp.sum(diagonal, axis=(0, 1), keepdims=True)
    whole = jnp.concatenate(
        [
            jnp.concatenate([own, jnp.transpose(left1), jnp.transpose(left2)], axis=1),
            jnp.concatenate([left1, c11, c12], axis=1),
            jnp.concatenate([left2, jnp.transpose(c12), c22], axis=1),
        ],
        axis=0,
    )
    return whole * (1.0 / size), size


def core_kernel(
    items, at_ref, near_ref, far_ref, wide_ref, weights_ref, place_ref,
    rows_ref, factors_ref, sums_ref, gram_ref, turn_t_ref, back_ref,
):
    piece = near_ref.shape[0]
    for k, ref in enumerate((near_ref, far_ref)):
        first = piece * (at_ref[0] if k == 0 else 1 - at_ref[0])
        sums_ref[pl.ds(pl.multiple_of(first, 8), piece), :] = ref[...]
    weights = weights_ref[...]
    whole, size = assemble(sums_ref, weights, items)
    gram_ref[...] = whole
    g = split(whole)

    x = whole[:RANK, :]
    first = tuple(part[:RANK, :] for part in g)
    h1 = mm_nt(first, first)
    low1, piv1 = eliminate(h1)
    x = turned(low1, piv1, x)
    x = mm(x, g)
    y = mm(x, g)
    h2 = mm_nt(x, y)
    low2, piv2 = eliminate(h2)
    x = turned(low2, piv2, y)
    x = mm(x, g)
    y = mm(x, g)
    h3 = mm_nt(x, y)
    low3, piv3 = eliminate(h3)
    turn_t_ref[...] = turned(low3, piv3, x)
    back_ref[...] = turned(low3, piv3, y)
    last = smallest(piv3, h3)
    fine = (smallest(piv1, h1) > 3e-5) & (smallest(piv2, h2) > 1e-5) & (last > 1e-4)

    @pl.when(jnp.logical_not(fine))
    def _():
        def turn(n, x):
            even = lax.rem(n, 2) == 0
            y = jnp.where(even, mm(x, split(gram_ref[...])), x)
            low, piv = eliminate(mm_nt(x, y))
            back = turned(low, piv, y)
            turn_t_ref[...] = turned(low, piv, x)
            back_ref[...] = back
            return back

        start = jnp.where(
            lax.broadcasted_iota(jnp.int32, (RANK, ORDER), 0) == lax.broadcasted_iota(jnp.int32, (RANK, ORDER), 1), 1.0, 0.0
        )
        lax.fori_loop(0, 9, turn, start)

    @pl.when(jnp.logical_not(fine & (last > 2e-2)))
    def _():
        x, y = polished(turn_t_ref[...], back_ref[...])
        turn_t_ref[...] = x
        back_ref[...] = y

    scale = lax.rsqrt(size)
    x = turn_t_ref[...] * scale
    left = split(jnp.concatenate([x[:, :RANK] * weights, x[:, RANK:]], axis=1))
    one = lambda a, b: lax.dot_general(a, b, (((1,), (1,)), ((), ())), preferred_element_type=f32)
    most = one(wide_ref[:, :ORDER], jnp.concatenate(left, axis=0))
    some = one(wide_ref[:, ORDER : ORDER + RANK], jnp.concatenate([p[:, :RANK] for p in left[:2]], axis=0))
    least = one(wide_ref[:, ORDER + RANK :], left[0][:, :RANK])
    strip = lambda y, k: y[:, RANK * k : RANK * (k + 1)]
    rows_ref[...] = strip(most, 0) + ((strip(most, 1) + strip(some, 0)) + (strip(most, 2) + strip(some, 1) + least))
    user_of = place_ref[...]
    onehot = jnp.where(lax.broadcasted_iota(jnp.int32, (USERS, USERS), 1) == user_of, 1.0, 0.0)
    factors_ref[...] = mm_nt(onehot, back_ref[:, RANK:] * (scale * size))


def core(at, near, far, wide, weights, place, items):
    in_vmem = pl.BlockSpec(memory_space=pltpu.VMEM)
    return pl.pallas_call(
        functools.partial(core_kernel, items),
        out_shape=[jax.ShapeDtypeStruct((wide.shape[0], RANK), f32), jax.ShapeDtypeStruct((USERS, RANK), f32)],
        in_specs=[pl.BlockSpec(memory_space=pltpu.SMEM)] + [in_vmem] * 5,
        scratch_shapes=[
            pltpu.VMEM((2 * ORDER, RANK), f32),
            pltpu.VMEM((ORDER, ORDER), f32),
            pltpu.VMEM((RANK, ORDER), f32),
            pltpu.VMEM((RANK, ORDER), f32),
        ],
        compiler_params=pltpu.CompilerParams(vmem_limit_bytes=32 * 2**20),
    )(at, near, far, wide, weights.reshape(1, RANK), place.reshape(-1, 1))


def column_kernel(row_ref, user_row_ref, blocks_ref, tiles_ref, out_ref):
    mine = user_row_ref[...] == row_ref[0]
    blocks = jnp.sum(jnp.where(mine, blocks_ref[...], 0), axis=1, keepdims=True)
    count = out_ref.shape[0]
    place = lax.broadcasted_iota(jnp.int32, (blocks.shape[0], count), 1) == blocks
    place = jnp.where(place, 1.0, 0.0).astype(jnp.bfloat16)
    dense = lax.dot_general(place, tiles_ref[...], (((0,), (0,)), ((), ())), preferred_element_type=f32)
    out_ref[...] = dense.astype(jnp.bfloat16)


def column_of(row, user_row, block_ids, tiles, count):
    in_vmem = pl.BlockSpec(memory_space=pltpu.VMEM)
    return pl.pallas_call(
        column_kernel,
        out_shape=jax.ShapeDtypeStruct((count, tiles.shape[1]), jnp.bfloat16),
        in_specs=[pl.BlockSpec(memory_space=pltpu.SMEM), in_vmem, in_vmem, in_vmem],
        out_specs=in_vmem,
    )(row.reshape(1), user_row.reshape(1, -1), block_ids.T, tiles)


def strips(at_ref, refs, flat_ref, users_ref):
    count = flat_ref.shape[0] // CAP
    owners = len(refs)
    for k, ref in enumerate(refs):
        flat_ref[...] = ref[...].astype(f32)
        blocks = [flat_ref[pl.ds(b, count, stride=CAP), :] for b in range(CAP)]
        owner = lax.rem(at_ref[2] + owners - k, owners)
        here = pl.ds(pl.multiple_of(owner * count, 16), count)
        users_ref[here, :] = jnp.concatenate(blocks, axis=1).astype(jnp.bfloat16)
    return users_ref[...]


def gram_kernel(at_ref, basis_ref, x0_ref, x1_ref, x2_ref, x3_ref, keep_ref, send_ref, flat_ref, users_ref, all_ref):
    x = strips(at_ref, (x0_ref, x1_ref, x2_ref, x3_ref), flat_ref, users_ref)
    parts = split(basis_ref[...])
    high_t, middle_t = (jnp.transpose(p.astype(f32)).astype(jnp.bfloat16) for p in parts[:2])
    one = lambda a, b: jnp.dot(a, b, preferred_element_type=f32)
    both = one(jnp.concatenate([x, high_t], axis=0), jnp.concatenate(parts, axis=1))
    strip = lambda rows, k: both[rows, RANK * k : RANK * (k + 1)]
    users, rest = slice(0, USERS), slice(USERS, None)
    small = strip(rest, 1) + strip(rest, 2)
    all_ref[:RANK, :] = strip(rest, 0) + (small + jnp.transpose(small) + one(middle_t, parts[1]))
    all_ref[RANK : 3 * RANK, :] = strip(users, 0) + (strip(users, 1) + strip(users, 2))
    cross = lax.dot_general(x, x, (((1,), (1,)), ((), ())), preferred_element_type=f32)
    all_ref[3 * RANK : 4 * RANK, :] = cross[:RANK, :RANK]
    all_ref[4 * RANK : 5 * RANK, :] = cross[:RANK, RANK:]
    all_ref[5 * RANK :, :] = cross[RANK:, RANK:]
    steps, piece = keep_ref.shape[:2]
    for half, ref in ((at_ref[0], keep_ref), (1 - at_ref[0], send_ref)):
        for k in range(steps):
            ring = lax.rem(at_ref[1] + k, steps)
            first = ((half * steps + ring) * 4 + at_ref[2]) * piece
            ref[k] = all_ref[pl.ds(pl.multiple_of(first, 8), piece), :]


def gram_parts(at, basis, pieces, steps):
    in_vmem = pl.BlockSpec(memory_space=pltpu.VMEM)
    piece = 6 * RANK // (2 * steps * len(pieces))
    return pl.pallas_call(
        gram_kernel,
        out_shape=[jax.ShapeDtypeStruct((steps, piece, RANK), f32)] * 2,
        in_specs=[pl.BlockSpec(memory_space=pltpu.SMEM)] + [in_vmem] * 5,
        scratch_shapes=[
            pltpu.VMEM(pieces[0].shape, f32),
            pltpu.VMEM((USERS, basis.shape[0]), jnp.bfloat16),
            pltpu.VMEM((6 * RANK, RANK), f32),
        ],
        compiler_params=pltpu.CompilerParams(vmem_limit_bytes=32 * 2**20),
    )(at, basis, *pieces)


def wide_kernel(at_ref, basis_ref, x0_ref, x1_ref, x2_ref, x3_ref, out_ref, flat_ref, users_ref):
    parts = split(basis_ref[...])
    x = strips(at_ref, (x0_ref, x1_ref, x2_ref, x3_ref), flat_ref, users_ref)
    out_ref[:, :RANK] = parts[0]
    out_ref[:, RANK:ORDER] = jnp.transpose(x.astype(f32)).astype(jnp.bfloat16)
    out_ref[:, ORDER : ORDER + RANK] = parts[1]
    out_ref[:, ORDER + RANK :] = parts[2]


def wide_of(at, basis, pieces):
    in_vmem = pl.BlockSpec(memory_space=pltpu.VMEM)
    return pl.pallas_call(
        wide_kernel,
        out_shape=jax.ShapeDtypeStruct((basis.shape[0], ORDER + 2 * RANK), jnp.bfloat16),
        in_specs=[pl.BlockSpec(memory_space=pltpu.SMEM)] + [in_vmem] * 5,
        scratch_shapes=[pltpu.VMEM(pieces[0].shape, f32), pltpu.VMEM((USERS, basis.shape[0]), jnp.bfloat16)],
        compiler_params=pltpu.CompilerParams(vmem_limit_bytes=32 * 2**20),
    )(at, basis, *pieces)


def around(x, axis):
    n = lax.axis_size(axis)
    return [lax.ppermute(x, axis, [(i, (i + k) % n) for i in range(n)]) for k in range(1, n)]


def copies(x, axes):
    x = jnp.broadcast_to(x, (lax.axis_size(axes), *x.shape))
    return lax.all_to_all(x, axes, split_axis=0, concat_axis=0, tiled=True)


def summed(keep, send):
    other = [(0, 1), (1, 0)]
    total = keep + lax.ppermute(send, "item_2", other)
    n = lax.axis_size("item_1")
    own = total[0]
    for k in range(1, n):
        own = own + lax.ppermute(total[k], "item_1", [(i, (i + k) % n) for i in range(n)])
    own = jnp.sum(copies(own, "item_0"), axis=0)
    half = copies(own, ("item_1", "user")).reshape(-1, RANK)
    return half, lax.ppermute(half, "item_2", other)


def per_device(basis, old_values, ratings, block_ids, user_row):
    n_item = lax.axis_size(ITEM)
    n_user = lax.axis_size("user")
    width = ratings.shape[2]
    slab_blocks = basis.shape[0] // width
    row = lax.axis_index(ITEM) * n_user + lax.axis_index("user")
    column = column_of(row, user_row, block_ids, ratings[0], n_item * slab_blocks)
    arrived = lax.all_to_all(column.reshape(n_item, slab_blocks, width), ITEM, 0, 0, tiled=True)
    arrived = arrived.reshape(n_item * slab_blocks, width)
    pieces = [arrived] + around(arrived, "user")
    places = [lax.axis_index(name) for name in ("item_2", "item_1", "user")]
    at = jnp.stack(places).astype(jnp.int32)
    keep, send = gram_parts(at, basis, pieces, lax.axis_size("item_1"))
    wide = wide_of(at, basis, pieces)
    near, far = summed(keep, send)
    place = user_row % n_user * n_item + user_row // n_user
    return tuple(core(at, near, far, wide, old_values, place, basis.shape[0] * n_item))


def solution(mesh):
    finer = Mesh(
        mesh.devices.reshape(8, 4, 2, mesh.shape["user"]), ("item_0", "item_1", "item_2", "user")
    )
    placed = (P(ITEM, None), P(), P(ITEM_USER, None, None), P(), P())
    return jax.shard_map(
        per_device, mesh=finer, in_specs=placed, out_specs=(P(ITEM, None), P()), check_vma=False
    )
```

```python
import functools

import jax
import jax.numpy as jnp
from jax import lax
from jax.experimental import pallas as pl
from jax.experimental.pallas import tpu as pltpu
from jax.sharding import Mesh
from jax.sharding import PartitionSpec as P

ITEM = ("item_0", "item_1", "item_2")
ITEM_USER = ("item_0", "item_1", "item_2", "user")

f32 = jnp.float32
RANK, USERS, ORDER, CAP = 128, 256, 384, 4


def split(x):
    high = x.astype(jnp.bfloat16)
    rest = x - high.astype(f32)
    middle = rest.astype(jnp.bfloat16)
    return high, middle, (rest - middle.astype(f32)).astype(jnp.bfloat16)


def product(a, b, dims):
    n = a[0].shape[0]
    one = lambda x, y: lax.dot_general(x, y, (dims, ((), ())), preferred_element_type=f32)
    p = one(jnp.concatenate(a, axis=0), b[0])
    q = one(jnp.concatenate(a[:2], axis=0), b[1])
    r = one(a[0], b[2])
    return p[:n] + ((p[n : 2 * n] + q[:n]) + ((p[2 * n :] + q[n:]) + r))


def mm(a, b):
    a = a if isinstance(a, tuple) else split(a)
    b = b if isinstance(b, tuple) else split(b)
    return product(a, b, ((1,), (0,)))


def mm_nt(a, b):
    a = a if isinstance(a, tuple) else split(a)
    b = b if isinstance(b, tuple) else split(b)
    return product(a, b, ((1,), (1,)))


def spread(x):
    return jnp.broadcast_to(x, (8, RANK))


def eliminate(gram):
    lane = lax.broadcasted_iota(jnp.int32, (8, RANK), 1)
    sub = lax.broadcasted_iota(jnp.int32, (8, RANK), 0)
    count = RANK // 8
    rows = [gram[8 * k : 8 * k + 8, :] for k in range(count)]
    pivots = []
    for panel in range(count):
        here = rows[panel]
        first = 8 * panel
        column = [spread(here[:, first + k : first + k + 1]) for k in range(8)]
        pivot_of_row = jnp.ones((8, RANK), f32)
        steps = []
        for s in range(0, 8, 2):
            upper = [spread(column[k][s : s + 1, :]) for k in range(s, 8)]
            under = [spread(column[k][s + 1 : s + 2, :]) for k in range(s + 1, 8)]
            a, b, c = upper[0], upper[1], under[0]
            det = a * c - b * b
            inverse = 1.0 / a
            second = 1.0 / det
            ratio = b * inverse
            line = spread(here[s : s + 1, :])
            line = jnp.where(lane == first + s, line + line, line)
            next_line = spread(here[s + 1 : s + 2, :]) - ratio * line
            next_line = jnp.where(lane == first + s + 1, next_line + next_line, next_line)
            pivot_of_row = jnp.where(sub == s, a, jnp.where(sub == s + 1, det * inverse, pivot_of_row))
            next_inverse, mixed = a * second, b * second
            under = [x - ratio * y for x, y in zip(under, upper[1:])]
            steps.append((inverse, line, upper))
            steps.append((next_inverse, next_line, under))
            one = jnp.where(sub > s, column[s] * inverse, 0.0)
            two = jnp.where(sub > s + 1, column[s + 1] * next_inverse - column[s] * mixed, 0.0)
            here = here - one * line - two * next_line
            for k in range(s + 2, 8):
                column[k] = column[k] - one * upper[k - s] - two * under[k - s - 1]
        rows[panel] = here
        pivots.append(pivot_of_row)
        for other in range(panel + 1, count):
            there = rows[other]
            column = [spread(there[:, first + k : first + k + 1]) for k in range(8)]
            for s, (inverse, line, upper) in enumerate(steps):
                factor = column[s] * inverse
                there = there - factor * line
                for k in range(s + 1, 8):
                    column[k] = column[k] - factor * upper[k - s]
            rows[other] = there
    return lower_of(jnp.concatenate(rows, axis=0)), jnp.concatenate(pivots, axis=0)


def square_iotas():
    i = lax.broadcasted_iota(jnp.int32, (RANK, RANK), 0)
    k = lax.broadcasted_iota(jnp.int32, (RANK, RANK), 1)
    return i, k


def lower_of(x):
    i, k = square_iotas()
    return jnp.where(i >= k, x, 0.0)


def scaled(x, pivots, power):
    factor = 1.0 / pivots if power == 1 else lax.rsqrt(pivots)
    return jnp.concatenate([x[:, c : c + RANK] * factor for c in range(0, x.shape[1], RANK)], axis=1)


def turned(lower, pivots, x):
    return scaled(mm(lower, scaled(x, pivots, 1)), pivots, 2)


def smallest(pivots, gram):
    i, k = square_iotas()
    start = jnp.sum(jnp.where(i == k, gram, 0.0), axis=1, keepdims=True)
    return jnp.min(pivots / start)


def polished(x, y):
    i, k = square_iotas()
    off = mm_nt(x, y) - jnp.where(i == k, 1.0, 0.0)
    step = jnp.where(i > k, off, jnp.where(i == k, 0.5 * off, 0.0))
    both = jnp.concatenate([x, y], axis=1)
    both = both - jnp.dot(step.astype(jnp.bfloat16), both.astype(jnp.bfloat16), preferred_element_type=f32)
    return both[:, :ORDER], both[:, ORDER:]


def assemble(sums, weights, items):
    i, k = square_iotas()
    block = lambda n: sums[RANK * n : RANK * (n + 1), :] * (1.0 / items)
    own = jnp.transpose(block(0) * weights) * weights
    left1, left2 = block(1) * weights, block(2) * weights
    c11, c12, c22 = block(3), block(4), block(5)
    diagonal = jnp.where(i == k, own + c11 + c22, 0.0)
    size = jnp.sum(diagonal, axis=(0, 1), keepdims=True)
    whole = jnp.concatenate(
        [
            jnp.concatenate([own, jnp.transpose(left1), jnp.transpose(left2)], axis=1),
            jnp.concatenate([left1, c11, c12], axis=1),
            jnp.concatenate([left2, jnp.transpose(c12), c22], axis=1),
        ],
        axis=0,
    )
    return whole * (1.0 / size), size


def core_kernel(
    items, sums_ref, wide_ref, weights_ref, place_ref, rows_ref, factors_ref, gram_ref, turn_t_ref, back_ref
):
    weights = weights_ref[...]
    whole, size = assemble(sums_ref, weights, items)
    gram_ref[...] = whole
    g = split(whole)

    x = whole[:RANK, :]
    first = tuple(part[:RANK, :] for part in g)
    h1 = mm_nt(first, first)
    low1, piv1 = eliminate(h1)
    x = turned(low1, piv1, x)
    x = mm(x, g)
    part = split(x)
    h2 = mm_nt(part, part)
    low2, piv2 = eliminate(h2)
    x = turned(low2, piv2, x)
    x = mm(x, g)
    x = mm(x, g)
    y = mm(x, g)
    h3 = mm_nt(x, y)
    low3, piv3 = eliminate(h3)
    turn_t_ref[...] = turned(low3, piv3, x)
    back_ref[...] = turned(low3, piv3, y)
    fine = (smallest(piv1, h1) > 3e-5) & (smallest(piv2, h2) > 1e-4) & (smallest(piv3, h3) > 5e-5)

    @pl.when(jnp.logical_not(fine))
    def _():
        def turn(n, x):
            even = lax.rem(n, 2) == 0
            y = jnp.where(even, mm(x, split(gram_ref[...])), x)
            low, piv = eliminate(mm_nt(x, y))
            back = turned(low, piv, y)
            turn_t_ref[...] = turned(low, piv, x)
            back_ref[...] = back
            return back

        start = jnp.where(
            lax.broadcasted_iota(jnp.int32, (RANK, ORDER), 0) == lax.broadcasted_iota(jnp.int32, (RANK, ORDER), 1), 1.0, 0.0
        )
        lax.fori_loop(0, 9, turn, start)

    x, y = polished(turn_t_ref[...], back_ref[...])
    scale = lax.rsqrt(size)
    x = x * scale
    left = split(jnp.concatenate([x[:, :RANK] * weights, x[:, RANK:]], axis=1))
    one = lambda a, b: lax.dot_general(a, b, (((1,), (1,)), ((), ())), preferred_element_type=f32)
    most = one(wide_ref[:, :ORDER], jnp.concatenate(left, axis=0))
    some = one(wide_ref[:, ORDER : ORDER + RANK], jnp.concatenate([p[:, :RANK] for p in left[:2]], axis=0))
    least = one(wide_ref[:, ORDER + RANK :], left[0][:, :RANK])
    strip = lambda y, k: y[:, RANK * k : RANK * (k + 1)]
    rows_ref[...] = strip(most, 0) + ((strip(most, 1) + strip(some, 0)) + (strip(most, 2) + strip(some, 1) + least))
    taken = lax.broadcasted_iota(jnp.int32, (USERS, USERS), 0) == place_ref[...]
    taken = jnp.where(taken, 1.0, 0.0).astype(jnp.bfloat16)
    parts = jnp.concatenate(split(y[:, RANK:] * (scale * size)), axis=0)
    found = jnp.dot(parts, taken, preferred_element_type=f32)
    found = found[:RANK] + (found[RANK : 2 * RANK] + found[2 * RANK :])
    factors_ref[...] = jnp.transpose(found)


def core(sums, wide, weights, place, items):
    in_vmem = pl.BlockSpec(memory_space=pltpu.VMEM)
    return pl.pallas_call(
        functools.partial(core_kernel, items),
        out_shape=[jax.ShapeDtypeStruct((wide.shape[0], RANK), f32), jax.ShapeDtypeStruct((USERS, RANK), f32)],
        in_specs=[in_vmem] * 4,
        scratch_shapes=[
            pltpu.VMEM((ORDER, ORDER), f32),
            pltpu.VMEM((RANK, ORDER), f32),
            pltpu.VMEM((RANK, ORDER), f32),
        ],
        compiler_params=pltpu.CompilerParams(vmem_limit_bytes=32 * 2**20),
    )(sums, wide, weights, place)


def column_kernel(n_user, row_ref, user_row_ref, blocks_ref, tiles_ref, weights_ref, out_ref, place_ref, same_ref):
    user_row = user_row_ref[...]
    mine = user_row == row_ref[0]
    blocks = jnp.sum(jnp.where(mine, blocks_ref[...], 0), axis=1, keepdims=True)
    count = out_ref.shape[0]
    place = lax.broadcasted_iota(jnp.int32, (blocks.shape[0], count), 1) == blocks
    place = jnp.where(place, 1.0, 0.0).astype(jnp.bfloat16)
    dense = lax.dot_general(place, tiles_ref[...], (((0,), (0,)), ((), ())), preferred_element_type=f32)
    out_ref[...] = dense.astype(jnp.bfloat16)
    place_ref[...] = lax.rem(user_row, n_user) * (user_row.shape[1] // n_user) + lax.div(user_row, n_user)
    same_ref[...] = weights_ref[...]


def column_of(row, user_row, block_ids, tiles, weights, count, n_user):
    in_vmem = pl.BlockSpec(memory_space=pltpu.VMEM)
    return pl.pallas_call(
        functools.partial(column_kernel, n_user),
        out_shape=[
            jax.ShapeDtypeStruct((count, tiles.shape[1]), jnp.bfloat16),
            jax.ShapeDtypeStruct((1, user_row.shape[0]), jnp.int32),
            jax.ShapeDtypeStruct((1, weights.shape[0]), f32),
        ],
        in_specs=[pl.BlockSpec(memory_space=pltpu.SMEM)] + [in_vmem] * 4,
    )(row.reshape(1), user_row.reshape(1, -1), block_ids.T, tiles, weights.reshape(1, -1))


def strips(at_ref, refs, flat_ref, users_ref):
    count = flat_ref.shape[0] // CAP
    owners = len(refs)
    for k, ref in enumerate(refs):
        flat_ref[...] = ref[...].astype(f32)
        blocks = [flat_ref[pl.ds(b, count, stride=CAP), :] for b in range(CAP)]
        owner = lax.rem(at_ref[0] + owners - k, owners)
        here = pl.ds(pl.multiple_of(owner * count, 16), count)
        users_ref[here, :] = jnp.concatenate(blocks, axis=1).astype(jnp.bfloat16)
    return users_ref[...]


def gram_kernel(at_ref, basis_ref, x0_ref, x1_ref, x2_ref, x3_ref, out_ref, flat_ref, users_ref, all_ref):
    x = strips(at_ref, (x0_ref, x1_ref, x2_ref, x3_ref), flat_ref, users_ref)
    parts = split(basis_ref[...])
    high_t, middle_t = (jnp.transpose(p.astype(f32)).astype(jnp.bfloat16) for p in parts[:2])
    one = lambda a, b: jnp.dot(a, b, preferred_element_type=f32)
    both = one(jnp.concatenate([x, high_t], axis=0), jnp.concatenate(parts, axis=1))
    strip = lambda rows, k: both[rows, RANK * k : RANK * (k + 1)]
    users, rest = slice(0, USERS), slice(USERS, None)
    small = strip(rest, 1) + strip(rest, 2)
    all_ref[:RANK, :] = strip(rest, 0) + (small + jnp.transpose(small) + one(middle_t, parts[1]))
    all_ref[RANK : 3 * RANK, :] = strip(users, 0) + (strip(users, 1) + strip(users, 2))
    cross = lax.dot_general(x, x, (((1,), (1,)), ((), ())), preferred_element_type=f32)
    all_ref[3 * RANK : 4 * RANK, :] = cross[:RANK, :RANK]
    all_ref[4 * RANK : 5 * RANK, :] = cross[:RANK, RANK:]
    all_ref[5 * RANK :, :] = cross[RANK:, RANK:]
    count, piece = out_ref.shape[:2]
    for k in range(count):
        first = (k * 4 + at_ref[0]) * piece
        out_ref[k] = all_ref[pl.ds(pl.multiple_of(first, 8), piece), :]


def gram_parts(at, basis, pieces, count):
    in_vmem = pl.BlockSpec(memory_space=pltpu.VMEM)
    return pl.pallas_call(
        gram_kernel,
        out_shape=jax.ShapeDtypeStruct((count, 6 * RANK // (count * len(pieces)), RANK), f32),
        in_specs=[pl.BlockSpec(memory_space=pltpu.SMEM)] + [in_vmem] * 5,
        scratch_shapes=[
            pltpu.VMEM(pieces[0].shape, f32),
            pltpu.VMEM((USERS, basis.shape[0]), jnp.bfloat16),
            pltpu.VMEM((6 * RANK, RANK), f32),
        ],
        compiler_params=pltpu.CompilerParams(vmem_limit_bytes=32 * 2**20),
    )(at, basis, *pieces)


def wide_kernel(at_ref, basis_ref, x0_ref, x1_ref, x2_ref, x3_ref, out_ref, flat_ref, users_ref):
    parts = split(basis_ref[...])
    x = strips(at_ref, (x0_ref, x1_ref, x2_ref, x3_ref), flat_ref, users_ref)
    out_ref[:, :RANK] = parts[0]
    out_ref[:, RANK:ORDER] = jnp.transpose(x.astype(f32)).astype(jnp.bfloat16)
    out_ref[:, ORDER : ORDER + RANK] = parts[1]
    out_ref[:, ORDER + RANK :] = parts[2]


def wide_of(at, basis, pieces):
    in_vmem = pl.BlockSpec(memory_space=pltpu.VMEM)
    return pl.pallas_call(
        wide_kernel,
        out_shape=jax.ShapeDtypeStruct((basis.shape[0], ORDER + 2 * RANK), jnp.bfloat16),
        in_specs=[pl.BlockSpec(memory_space=pltpu.SMEM)] + [in_vmem] * 5,
        scratch_shapes=[pltpu.VMEM(pieces[0].shape, f32), pltpu.VMEM((USERS, basis.shape[0]), jnp.bfloat16)],
        compiler_params=pltpu.CompilerParams(vmem_limit_bytes=32 * 2**20),
    )(at, basis, *pieces)


def around(x, axis):
    n = lax.axis_size(axis)
    return [lax.ppermute(x, axis, [(i, (i + k) % n) for i in range(n)]) for k in range(1, n)]


def copies(x, axes):
    x = jnp.broadcast_to(x, (lax.axis_size(axes), *x.shape))
    return lax.all_to_all(x, axes, split_axis=0, concat_axis=0, tiled=True)


def summed(parts):
    near = ("item_1", "item_2")
    own = jnp.sum(lax.all_to_all(parts, near, 0, 0, tiled=True), axis=0)
    own = jnp.sum(copies(own, "item_0"), axis=0)
    return copies(own, (*near, "user")).reshape(-1, RANK)


def per_device(basis, old_values, ratings, block_ids, user_row):
    n_item = lax.axis_size(ITEM)
    n_user = lax.axis_size("user")
    width = ratings.shape[2]
    slab_blocks = basis.shape[0] // width
    user = lax.axis_index("user")
    row = lax.axis_index(ITEM) * n_user + user
    at = user.reshape(1)
    column, place, weights = column_of(row, user_row, block_ids, ratings[0], old_values, n_item * slab_blocks, n_user)
    arrived = lax.all_to_all(column.reshape(n_item, slab_blocks, width), ITEM, 0, 0, tiled=True)
    arrived = arrived.reshape(n_item * slab_blocks, width)
    pieces = [arrived] + around(arrived, "user")
    parts = gram_parts(at, basis, pieces, lax.axis_size("item_1") * lax.axis_size("item_2"))
    wide = wide_of(at, basis, pieces)
    return tuple(core(summed(parts), wide, weights, place, basis.shape[0] * n_item))


def solution(mesh):
    finer = Mesh(
        mesh.devices.reshape(8, 4, 2, mesh.shape["user"]), ("item_0", "item_1", "item_2", "user")
    )
    placed = (P(ITEM, None), P(), P(ITEM_USER, None, None), P(), P())
    return jax.shard_map(
        per_device, mesh=finer, in_specs=placed, out_specs=(P(ITEM, None), P()), check_vma=False
    )
```

```python
import functools

import jax
import jax.numpy as jnp
from jax import lax
from jax.experimental import pallas as pl
from jax.experimental.pallas import tpu as pltpu
from jax.sharding import Mesh
from jax.sharding import PartitionSpec as P

ITEM = ("item_0", "item_1", "item_2")
ITEM_USER = ("item_0", "item_1", "item_2", "user")

f32 = jnp.float32
RANK, USERS, ORDER, CAP = 128, 256, 384, 4


def split(x):
    high = x.astype(jnp.bfloat16)
    rest = x - high.astype(f32)
    middle = rest.astype(jnp.bfloat16)
    return high, middle, (rest - middle.astype(f32)).astype(jnp.bfloat16)


def product(a, b, dims):
    n = a[0].shape[0]
    one = lambda x, y: lax.dot_general(x, y, (dims, ((), ())), preferred_element_type=f32)
    p = one(jnp.concatenate(a, axis=0), b[0])
    q = one(jnp.concatenate(a[:2], axis=0), b[1])
    r = one(a[0], b[2])
    return p[:n] + ((p[n : 2 * n] + q[:n]) + ((p[2 * n :] + q[n:]) + r))


def mm(a, b):
    a = a if isinstance(a, tuple) else split(a)
    b = b if isinstance(b, tuple) else split(b)
    return product(a, b, ((1,), (0,)))


def mm_nt(a, b):
    a = a if isinstance(a, tuple) else split(a)
    b = b if isinstance(b, tuple) else split(b)
    return product(a, b, ((1,), (1,)))


def spread(x):
    return jnp.broadcast_to(x, (8, RANK))


def eliminate(gram):
    lane = lax.broadcasted_iota(jnp.int32, (8, RANK), 1)
    sub = lax.broadcasted_iota(jnp.int32, (8, RANK), 0)
    count = RANK // 8
    rows = [gram[8 * k : 8 * k + 8, :] for k in range(count)]
    pivots = []
    for panel in range(count):
        here = rows[panel]
        first = 8 * panel
        column = [spread(here[:, first + k : first + k + 1]) for k in range(8)]
        pivot_of_row = jnp.ones((8, RANK), f32)
        steps = []
        for s in range(0, 8, 2):
            upper = [spread(column[k][s : s + 1, :]) for k in range(s, 8)]
            under = [spread(column[k][s + 1 : s + 2, :]) for k in range(s + 1, 8)]
            a, b, c = upper[0], upper[1], under[0]
            det = a * c - b * b
            inverse = 1.0 / a
            second = 1.0 / det
            ratio = b * inverse
            line = spread(here[s : s + 1, :])
            line = jnp.where(lane == first + s, line + line, line)
            next_line = spread(here[s + 1 : s + 2, :]) - ratio * line
            next_line = jnp.where(lane == first + s + 1, next_line + next_line, next_line)
            pivot_of_row = jnp.where(sub == s, a, jnp.where(sub == s + 1, det * inverse, pivot_of_row))
            next_inverse, mixed = a * second, b * second
            under = [x - ratio * y for x, y in zip(under, upper[1:])]
            steps.append((inverse, line, upper))
            steps.append((next_inverse, next_line, under))
            one = jnp.where(sub > s, column[s] * inverse, 0.0)
            two = jnp.where(sub > s + 1, column[s + 1] * next_inverse - column[s] * mixed, 0.0)
            here = here - one * line - two * next_line
            for k in range(s + 2, 8):
                column[k] = column[k] - one * upper[k - s] - two * under[k - s - 1]
        rows[panel] = here
        pivots.append(pivot_of_row)
        for other in range(panel + 1, min(panel + 2, count)):
            there = rows[other]
            column = [spread(there[:, first + k : first + k + 1]) for k in range(8)]
            for s, (inverse, line, upper) in enumerate(steps):
                factor = column[s] * inverse
                there = there - factor * line
                for k in range(s + 1, 8):
                    column[k] = column[k] - factor * upper[k - s]
            rows[other] = there
        solved = [None] * 8
        for s in range(7, -1, -1):
            inverse, line, upper = steps[s]
            for k in range(s + 1, 8):
                line = line - upper[k - s] * solved[k]
            solved[s] = line * inverse
        for other in range(panel + 2, count):
            there = rows[other]
            for k in range(8):
                there = there - spread(rows[other][:, first + k : first + k + 1]) * solved[k]
            rows[other] = there
    return lower_of(jnp.concatenate(rows, axis=0)), jnp.concatenate(pivots, axis=0)


def square_iotas():
    i = lax.broadcasted_iota(jnp.int32, (RANK, RANK), 0)
    k = lax.broadcasted_iota(jnp.int32, (RANK, RANK), 1)
    return i, k


def lower_of(x):
    i, k = square_iotas()
    return jnp.where(i >= k, x, 0.0)


def scaled(x, pivots, power):
    factor = 1.0 / pivots if power == 1 else lax.rsqrt(pivots)
    return jnp.concatenate([x[:, c : c + RANK] * factor for c in range(0, x.shape[1], RANK)], axis=1)


def turned(lower, pivots, x):
    return scaled(mm(lower, scaled(x, pivots, 1)), pivots, 2)


def smallest(pivots, gram):
    i, k = square_iotas()
    start = jnp.sum(jnp.where(i == k, gram, 0.0), axis=1, keepdims=True)
    return jnp.min(pivots / start)


def polished(x, y):
    i, k = square_iotas()
    off = mm_nt(x, y) - jnp.where(i == k, 1.0, 0.0)
    step = jnp.where(i > k, off, jnp.where(i == k, 0.5 * off, 0.0))
    both = jnp.concatenate([x, y], axis=1)
    both = both - jnp.dot(step.astype(jnp.bfloat16), both.astype(jnp.bfloat16), preferred_element_type=f32)
    return both[:, :ORDER], both[:, ORDER:]


def assemble(sums, weights, items):
    i, k = square_iotas()
    block = lambda n: sums[RANK * n : RANK * (n + 1), :] * (1.0 / items)
    own = jnp.transpose(block(0) * weights) * weights
    left1, left2 = block(1) * weights, block(2) * weights
    c11, c12, c22 = block(3), block(4), block(5)
    diagonal = jnp.where(i == k, own + c11 + c22, 0.0)
    size = jnp.sum(diagonal, axis=(0, 1), keepdims=True)
    whole = jnp.concatenate(
        [
            jnp.concatenate([own, jnp.transpose(left1), jnp.transpose(left2)], axis=1),
            jnp.concatenate([left1, c11, c12], axis=1),
            jnp.concatenate([left2, jnp.transpose(c12), c22], axis=1),
        ],
        axis=0,
    )
    return whole * (1.0 / size), size


def core_kernel(
    items, at_ref, near_ref, far_ref, wide_ref, weights_ref, place_ref,
    rows_ref, factors_ref, sums_ref, gram_ref, turn_t_ref, back_ref,
):
    half = near_ref.shape[0]
    for place, ref in ((at_ref[1], near_ref), (1 - at_ref[1], far_ref)):
        sums_ref[pl.ds(pl.multiple_of(place * half, 8), half), :] = ref[...]
    weights = weights_ref[...]
    whole, size = assemble(sums_ref, weights, items)
    gram_ref[...] = whole
    g = split(whole)

    x = whole[:RANK, :]
    first = tuple(part[:RANK, :] for part in g)
    h1 = mm_nt(first, first)
    low1, piv1 = eliminate(h1)
    x = turned(low1, piv1, x)
    x = mm(x, g)
    part = split(x)
    h2 = mm_nt(part, part)
    low2, piv2 = eliminate(h2)
    x = turned(low2, piv2, x)
    x = mm(x, g)
    x = mm(x, g)
    y = mm(x, g)
    h3 = mm_nt(x, y)
    low3, piv3 = eliminate(h3)
    turn_t_ref[...] = turned(low3, piv3, x)
    back_ref[...] = turned(low3, piv3, y)
    fine = (smallest(piv1, h1) > 3e-5) & (smallest(piv2, h2) > 1e-4) & (smallest(piv3, h3) > 5e-5)

    @pl.when(jnp.logical_not(fine))
    def _():
        def turn(n, x):
            even = lax.rem(n, 2) == 0
            y = jnp.where(even, mm(x, split(gram_ref[...])), x)
            low, piv = eliminate(mm_nt(x, y))
            back = turned(low, piv, y)
            turn_t_ref[...] = turned(low, piv, x)
            back_ref[...] = back
            return back

        start = jnp.where(
            lax.broadcasted_iota(jnp.int32, (RANK, ORDER), 0) == lax.broadcasted_iota(jnp.int32, (RANK, ORDER), 1), 1.0, 0.0
        )
        lax.fori_loop(0, 9, turn, start)

    x, y = polished(turn_t_ref[...], back_ref[...])
    scale = lax.rsqrt(size)
    x = x * scale
    left = split(jnp.concatenate([x[:, :RANK] * weights, x[:, RANK:]], axis=1))
    one = lambda a, b: lax.dot_general(a, b, (((1,), (1,)), ((), ())), preferred_element_type=f32)
    most = one(wide_ref[:, :ORDER], jnp.concatenate(left, axis=0))
    some = one(wide_ref[:, ORDER : ORDER + RANK], jnp.concatenate([p[:, :RANK] for p in left[:2]], axis=0))
    least = one(wide_ref[:, ORDER + RANK :], left[0][:, :RANK])
    strip = lambda y, k: y[:, RANK * k : RANK * (k + 1)]
    rows_ref[...] = strip(most, 0) + ((strip(most, 1) + strip(some, 0)) + (strip(most, 2) + strip(some, 1) + least))
    taken = lax.broadcasted_iota(jnp.int32, (USERS, USERS), 0) == place_ref[...]
    taken = jnp.where(taken, 1.0, 0.0).astype(jnp.bfloat16)
    parts = jnp.concatenate(split(y[:, RANK:] * (scale * size)), axis=0)
    found = jnp.dot(parts, taken, preferred_element_type=f32)
    found = found[:RANK] + (found[RANK : 2 * RANK] + found[2 * RANK :])
    factors_ref[...] = jnp.transpose(found)


def core(at, near, far, wide, weights, place, items):
    in_vmem = pl.BlockSpec(memory_space=pltpu.VMEM)
    return pl.pallas_call(
        functools.partial(core_kernel, items),
        out_shape=[jax.ShapeDtypeStruct((wide.shape[0], RANK), f32), jax.ShapeDtypeStruct((USERS, RANK), f32)],
        in_specs=[pl.BlockSpec(memory_space=pltpu.SMEM)] + [in_vmem] * 5,
        scratch_shapes=[
            pltpu.VMEM((2 * ORDER, RANK), f32),
            pltpu.VMEM((ORDER, ORDER), f32),
            pltpu.VMEM((RANK, ORDER), f32),
            pltpu.VMEM((RANK, ORDER), f32),
        ],
        compiler_params=pltpu.CompilerParams(vmem_limit_bytes=32 * 2**20),
    )(at, near, far, wide, weights, place)


def column_kernel(row_ref, user_row_ref, blocks_ref, tiles_ref, out_ref):
    mine = user_row_ref[...] == row_ref[0]
    blocks = jnp.sum(jnp.where(mine, blocks_ref[...], 0), axis=1, keepdims=True)
    count = out_ref.shape[0]
    place = lax.broadcasted_iota(jnp.int32, (blocks.shape[0], count), 1) == blocks
    place = jnp.where(place, 1.0, 0.0).astype(jnp.bfloat16)
    dense = lax.dot_general(place, tiles_ref[...], (((0,), (0,)), ((), ())), preferred_element_type=f32)
    out_ref[...] = dense.astype(jnp.bfloat16)


def column_of(row, user_row, block_ids, tiles, count):
    in_vmem = pl.BlockSpec(memory_space=pltpu.VMEM)
    return pl.pallas_call(
        column_kernel,
        out_shape=jax.ShapeDtypeStruct((count, tiles.shape[1]), jnp.bfloat16),
        in_specs=[pl.BlockSpec(memory_space=pltpu.SMEM)] + [in_vmem] * 3,
    )(row.reshape(1), user_row.reshape(1, -1), block_ids.T, tiles)


def strips(at_ref, refs, flat_ref, users_ref):
    count = flat_ref.shape[0] // CAP
    owners = len(refs)
    for k, ref in enumerate(refs):
        flat_ref[...] = ref[...].astype(f32)
        blocks = [flat_ref[pl.ds(b, count, stride=CAP), :] for b in range(CAP)]
        owner = lax.rem(at_ref[0] + owners - k, owners)
        here = pl.ds(pl.multiple_of(owner * count, 16), count)
        users_ref[here, :] = jnp.concatenate(blocks, axis=1).astype(jnp.bfloat16)
    return users_ref[...]


def gram_kernel(at_ref, basis_ref, x0_ref, x1_ref, x2_ref, x3_ref, out_ref, flat_ref, users_ref, all_ref):
    x = strips(at_ref, (x0_ref, x1_ref, x2_ref, x3_ref), flat_ref, users_ref)
    parts = split(basis_ref[...])
    high_t, middle_t = (jnp.transpose(p.astype(f32)).astype(jnp.bfloat16) for p in parts[:2])
    one = lambda a, b: jnp.dot(a, b, preferred_element_type=f32)
    both = one(jnp.concatenate([x, high_t], axis=0), jnp.concatenate(parts, axis=1))
    strip = lambda rows, k: both[rows, RANK * k : RANK * (k + 1)]
    users, rest = slice(0, USERS), slice(USERS, None)
    small = strip(rest, 1) + strip(rest, 2)
    all_ref[:RANK, :] = strip(rest, 0) + (small + jnp.transpose(small) + one(middle_t, parts[1]))
    all_ref[RANK : 3 * RANK, :] = strip(users, 0) + (strip(users, 1) + strip(users, 2))
    cross = lax.dot_general(x, x, (((1,), (1,)), ((), ())), preferred_element_type=f32)
    all_ref[3 * RANK : 4 * RANK, :] = cross[:RANK, :RANK]
    all_ref[4 * RANK : 5 * RANK, :] = cross[:RANK, RANK:]
    all_ref[5 * RANK :, :] = cross[RANK:, RANK:]
    count, piece = out_ref.shape[:2]
    for k in range(count):
        first = (k * 4 + at_ref[0]) * piece
        out_ref[k] = all_ref[pl.ds(pl.multiple_of(first, 8), piece), :]


def gram_parts(at, basis, pieces, count):
    in_vmem = pl.BlockSpec(memory_space=pltpu.VMEM)
    return pl.pallas_call(
        gram_kernel,
        out_shape=jax.ShapeDtypeStruct((count, 6 * RANK // (count * len(pieces)), RANK), f32),
        in_specs=[pl.BlockSpec(memory_space=pltpu.SMEM)] + [in_vmem] * 5,
        scratch_shapes=[
            pltpu.VMEM(pieces[0].shape, f32),
            pltpu.VMEM((USERS, basis.shape[0]), jnp.bfloat16),
            pltpu.VMEM((6 * RANK, RANK), f32),
        ],
        compiler_params=pltpu.CompilerParams(vmem_limit_bytes=32 * 2**20),
    )(at, basis, *pieces)


def wide_kernel(
    at_ref, basis_ref, x0_ref, x1_ref, x2_ref, x3_ref, user_row_ref, weights_ref,
    out_ref, place_ref, same_ref, flat_ref, users_ref, row_ref, sems,
):
    fetch = pltpu.make_async_copy(user_row_ref, row_ref, sems.at[0])
    hand_on = pltpu.make_async_copy(weights_ref, same_ref, sems.at[1])
    fetch.start()
    hand_on.start()
    parts = split(basis_ref[...])
    x = strips(at_ref, (x0_ref, x1_ref, x2_ref, x3_ref), flat_ref, users_ref)
    out_ref[:, :RANK] = parts[0]
    out_ref[:, RANK:ORDER] = jnp.transpose(x.astype(f32)).astype(jnp.bfloat16)
    out_ref[:, ORDER : ORDER + RANK] = parts[1]
    out_ref[:, ORDER + RANK :] = parts[2]
    fetch.wait()
    hand_on.wait()
    user_row = row_ref[...]
    place_ref[...] = lax.rem(user_row, 4) * (user_row.shape[1] // 4) + lax.div(user_row, 4)


def wide_of(at, basis, pieces, user_row, weights):
    in_vmem, in_hbm = pl.BlockSpec(memory_space=pltpu.VMEM), pl.BlockSpec(memory_space=pltpu.HBM)
    users = user_row.shape[0]
    return pl.pallas_call(
        wide_kernel,
        out_shape=[
            jax.ShapeDtypeStruct((basis.shape[0], ORDER + 2 * RANK), jnp.bfloat16),
            jax.ShapeDtypeStruct((1, users), jnp.int32),
            jax.ShapeDtypeStruct((1, RANK), f32),
        ],
        in_specs=[pl.BlockSpec(memory_space=pltpu.SMEM)] + [in_vmem] * 5 + [in_hbm] * 2,
        out_specs=[in_vmem] * 3,
        scratch_shapes=[
            pltpu.VMEM(pieces[0].shape, f32),
            pltpu.VMEM((users, basis.shape[0]), jnp.bfloat16),
            pltpu.VMEM((1, users), jnp.int32),
            pltpu.SemaphoreType.DMA((2,)),
        ],
        compiler_params=pltpu.CompilerParams(vmem_limit_bytes=32 * 2**20),
    )(at, basis, *pieces, user_row.reshape(1, -1), weights.reshape(1, -1))


def around(x, axis):
    n = lax.axis_size(axis)
    return [lax.ppermute(x, axis, [(i, (i + k) % n) for i in range(n)]) for k in range(1, n)]


def copies(x, axes):
    x = jnp.broadcast_to(x, (lax.axis_size(axes), *x.shape))
    return lax.all_to_all(x, axes, split_axis=0, concat_axis=0, tiled=True)


def summed(parts):
    own = jnp.sum(lax.all_to_all(parts, ("item_2", "item_1"), 0, 0, tiled=True), axis=0)
    own = jnp.sum(copies(own, "item_0"), axis=0)
    half = copies(own, ("item_1", "user")).reshape(-1, RANK)
    return half, lax.ppermute(half, "item_2", [(0, 1), (1, 0)])


def per_device(basis, old_values, ratings, block_ids, user_row):
    n_item = lax.axis_size(ITEM)
    width = ratings.shape[2]
    slab_blocks = basis.shape[0] // width
    user = lax.axis_index("user")
    row = lax.axis_index(ITEM) * lax.axis_size("user") + user
    at = jnp.stack([user, lax.axis_index("item_2")]).astype(jnp.int32)
    column = column_of(row, user_row, block_ids, ratings[0], n_item * slab_blocks)
    arrived = lax.all_to_all(column.reshape(n_item, slab_blocks, width), ITEM, 0, 0, tiled=True)
    arrived = arrived.reshape(n_item * slab_blocks, width)
    pieces = [arrived] + around(arrived, "user")
    parts = gram_parts(at, basis, pieces, lax.axis_size("item_1") * lax.axis_size("item_2"))
    wide, place, weights = wide_of(at, basis, pieces, user_row, old_values)
    near, far = summed(parts)
    return tuple(core(at, near, far, wide, weights, place, basis.shape[0] * n_item))


def solution(mesh):
    finer = Mesh(
        mesh.devices.reshape(8, 4, 2, mesh.shape["user"]), ("item_0", "item_1", "item_2", "user")
    )
    placed = (P(ITEM, None), P(), P(ITEM_USER, None, None), P(), P())
    return jax.shard_map(
        per_device, mesh=finer, in_specs=placed, out_specs=(P(ITEM, None), P()), check_vma=False
    )
```

```python
import functools

import jax
import jax.numpy as jnp
from jax import lax
from jax.experimental import pallas as pl
from jax.experimental.pallas import tpu as pltpu
from jax.sharding import Mesh
from jax.sharding import PartitionSpec as P

ITEM = ("item_0", "item_1", "item_2")
ITEM_USER = ("item_0", "item_1", "item_2", "user")

f32 = jnp.float32
RANK, USERS, ORDER, CAP = 128, 256, 384, 4


def split(x):
    high = x.astype(jnp.bfloat16)
    rest = x - high.astype(f32)
    middle = rest.astype(jnp.bfloat16)
    return high, middle, (rest - middle.astype(f32)).astype(jnp.bfloat16)


def product(a, b, dims):
    n = a[0].shape[0]
    one = lambda x, y: lax.dot_general(x, y, (dims, ((), ())), preferred_element_type=f32)
    p = one(jnp.concatenate(a, axis=0), b[0])
    q = one(jnp.concatenate(a[:2], axis=0), b[1])
    r = one(a[0], b[2])
    return p[:n] + ((p[n : 2 * n] + q[:n]) + ((p[2 * n :] + q[n:]) + r))


def mm(a, b):
    a = a if isinstance(a, tuple) else split(a)
    b = b if isinstance(b, tuple) else split(b)
    return product(a, b, ((1,), (0,)))


def mm_nt(a, b):
    a = a if isinstance(a, tuple) else split(a)
    b = b if isinstance(b, tuple) else split(b)
    return product(a, b, ((1,), (1,)))


def spread(x):
    return jnp.broadcast_to(x, (8, RANK))


def eliminate(gram):
    lane = lax.broadcasted_iota(jnp.int32, (8, RANK), 1)
    sub = lax.broadcasted_iota(jnp.int32, (8, RANK), 0)
    count = RANK // 8
    rows = [gram[8 * k : 8 * k + 8, :] for k in range(count)]
    pivots = []
    for panel in range(count):
        here = rows[panel]
        first = 8 * panel
        column = [spread(here[:, first + k : first + k + 1]) for k in range(8)]
        pivot_of_row = jnp.ones((8, RANK), f32)
        steps = []
        for s in range(0, 8, 2):
            upper = [spread(column[k][s : s + 1, :]) for k in range(s, 8)]
            under = [spread(column[k][s + 1 : s + 2, :]) for k in range(s + 1, 8)]
            a, b, c = upper[0], upper[1], under[0]
            det = a * c - b * b
            inverse = 1.0 / a
            second = 1.0 / det
            ratio = b * inverse
            line = spread(here[s : s + 1, :])
            line = jnp.where(lane == first + s, line + line, line)
            next_line = spread(here[s + 1 : s + 2, :]) - ratio * line
            next_line = jnp.where(lane == first + s + 1, next_line + next_line, next_line)
            pivot_of_row = jnp.where(sub == s, a, jnp.where(sub == s + 1, det * inverse, pivot_of_row))
            next_inverse, mixed = a * second, b * second
            under = [x - ratio * y for x, y in zip(under, upper[1:])]
            steps.append((inverse, line, upper))
            steps.append((next_inverse, next_line, under))
            one = jnp.where(sub > s, column[s] * inverse, 0.0)
            two = jnp.where(sub > s + 1, column[s + 1] * next_inverse - column[s] * mixed, 0.0)
            here = here - one * line - two * next_line
            for k in range(s + 2, 8):
                column[k] = column[k] - one * upper[k - s] - two * under[k - s - 1]
        rows[panel] = here
        pivots.append(pivot_of_row)
        for other in range(panel + 1, min(panel + 2, count)):
            there = rows[other]
            column = [spread(there[:, first + k : first + k + 1]) for k in range(8)]
            for s, (inverse, line, upper) in enumerate(steps):
                factor = column[s] * inverse
                there = there - factor * line
                for k in range(s + 1, 8):
                    column[k] = column[k] - factor * upper[k - s]
            rows[other] = there
        solved = [None] * 8
        for s in range(7, -1, -1):
            inverse, line, upper = steps[s]
            for k in range(s + 1, 8):
                line = line - upper[k - s] * solved[k]
            solved[s] = line * inverse
        for other in range(panel + 2, count):
            there = rows[other]
            for k in range(8):
                there = there - spread(rows[other][:, first + k : first + k + 1]) * solved[k]
            rows[other] = there
    return lower_of(jnp.concatenate(rows, axis=0)), jnp.concatenate(pivots, axis=0)


def square_iotas():
    i = lax.broadcasted_iota(jnp.int32, (RANK, RANK), 0)
    k = lax.broadcasted_iota(jnp.int32, (RANK, RANK), 1)
    return i, k


def lower_of(x):
    i, k = square_iotas()
    return jnp.where(i >= k, x, 0.0)


def scaled(x, pivots, power):
    factor = 1.0 / pivots if power == 1 else lax.rsqrt(pivots)
    return jnp.concatenate([x[:, c : c + RANK] * factor for c in range(0, x.shape[1], RANK)], axis=1)


def turned(lower, pivots, x):
    return scaled(mm(lower, scaled(x, pivots, 1)), pivots, 2)


def smallest(pivots, gram):
    i, k = square_iotas()
    start = jnp.sum(jnp.where(i == k, gram, 0.0), axis=1, keepdims=True)
    return jnp.min(pivots / start)


def polished(x, y):
    i, k = square_iotas()
    off = mm_nt(x, y) - jnp.where(i == k, 1.0, 0.0)
    step = jnp.where(i > k, off, jnp.where(i == k, 0.5 * off, 0.0))
    both = jnp.concatenate([x, y], axis=1)
    both = both - jnp.dot(step.astype(jnp.bfloat16), both.astype(jnp.bfloat16), preferred_element_type=f32)
    return both[:, :ORDER], both[:, ORDER:]


def assemble(sums, weights, items):
    i, k = square_iotas()
    block = lambda n: sums[RANK * n : RANK * (n + 1), :] * (1.0 / items)
    own = jnp.transpose(block(0) * weights) * weights
    left1, left2 = block(1) * weights, block(2) * weights
    c11, c12, c22 = block(3), block(4), block(5)
    diagonal = jnp.where(i == k, own + c11 + c22, 0.0)
    size = jnp.sum(diagonal, axis=(0, 1), keepdims=True)
    whole = jnp.concatenate(
        [
            jnp.concatenate([own, jnp.transpose(left1), jnp.transpose(left2)], axis=1),
            jnp.concatenate([left1, c11, c12], axis=1),
            jnp.concatenate([left2, jnp.transpose(c12), c22], axis=1),
        ],
        axis=0,
    )
    return whole * (1.0 / size), size


def core_kernel(
    items, core_ref, near_ref, far_ref, wide_ref, weights_ref, place_ref,
    rows_ref, factors_ref, sums_ref, gram_ref, turn_t_ref, back_ref,
):
    half = near_ref.shape[0]
    for place, ref in ((core_ref[0], near_ref), (1 - core_ref[0], far_ref)):
        sums_ref[pl.ds(pl.multiple_of(place * half, 8), half), :] = ref[...]
    weights = weights_ref[...]
    whole, size = assemble(sums_ref, weights, items)
    gram_ref[...] = whole
    g = split(whole)

    x = whole[:RANK, :]
    first = tuple(part[:RANK, :] for part in g)
    h1 = mm_nt(first, first)
    low1, piv1 = eliminate(h1)
    x = turned(low1, piv1, x)
    x = mm(x, g)
    part = split(x)
    h2 = mm_nt(part, part)
    low2, piv2 = eliminate(h2)
    x = turned(low2, piv2, x)
    x = mm(x, g)
    x = mm(x, g)
    y = mm(x, g)
    h3 = mm_nt(x, y)
    low3, piv3 = eliminate(h3)
    turn_t_ref[...] = turned(low3, piv3, x)
    back_ref[...] = turned(low3, piv3, y)
    fine = (smallest(piv1, h1) > 3e-5) & (smallest(piv2, h2) > 1e-4) & (smallest(piv3, h3) > 5e-5)

    @pl.when(jnp.logical_not(fine))
    def _():
        def turn(n, x):
            even = lax.rem(n, 2) == 0
            y = jnp.where(even, mm(x, split(gram_ref[...])), x)
            low, piv = eliminate(mm_nt(x, y))
            back = turned(low, piv, y)
            turn_t_ref[...] = turned(low, piv, x)
            back_ref[...] = back
            return back

        start = jnp.where(
            lax.broadcasted_iota(jnp.int32, (RANK, ORDER), 0) == lax.broadcasted_iota(jnp.int32, (RANK, ORDER), 1), 1.0, 0.0
        )
        lax.fori_loop(0, 9, turn, start)

    x, y = polished(turn_t_ref[...], back_ref[...])
    scale = lax.rsqrt(size)
    x = x * scale
    left = split(jnp.concatenate([x[:, :RANK] * weights, x[:, RANK:]], axis=1))
    one = lambda a, b: lax.dot_general(a, b, (((1,), (1,)), ((), ())), preferred_element_type=f32)
    most = one(wide_ref[:, :ORDER], jnp.concatenate(left, axis=0))
    some = one(wide_ref[:, ORDER : ORDER + RANK], jnp.concatenate([p[:, :RANK] for p in left[:2]], axis=0))
    least = one(wide_ref[:, ORDER + RANK :], left[0][:, :RANK])
    strip = lambda y, k: y[:, RANK * k : RANK * (k + 1)]
    rows_ref[...] = strip(most, 0) + ((strip(most, 1) + strip(some, 0)) + (strip(most, 2) + strip(some, 1) + least))
    taken = lax.broadcasted_iota(jnp.int32, (USERS, USERS), 0) == place_ref[...]
    taken = jnp.where(taken, 1.0, 0.0).astype(jnp.bfloat16)
    parts = jnp.concatenate(split(y[:, RANK:] * (scale * size)), axis=0)
    found = jnp.dot(parts, taken, preferred_element_type=f32)
    found = found[:RANK] + (found[RANK : 2 * RANK] + found[2 * RANK :])
    factors_ref[...] = jnp.transpose(found)


def core(here, near, far, wide, weights, place, items):
    in_vmem = pl.BlockSpec(memory_space=pltpu.VMEM)
    return pl.pallas_call(
        functools.partial(core_kernel, items),
        out_shape=[jax.ShapeDtypeStruct((wide.shape[0], RANK), f32), jax.ShapeDtypeStruct((USERS, RANK), f32)],
        in_specs=[pl.BlockSpec(memory_space=pltpu.SMEM)] + [in_vmem] * 5,
        scratch_shapes=[
            pltpu.VMEM((2 * ORDER, RANK), f32),
            pltpu.VMEM((ORDER, ORDER), f32),
            pltpu.VMEM((RANK, ORDER), f32),
            pltpu.VMEM((RANK, ORDER), f32),
        ],
        compiler_params=pltpu.CompilerParams(vmem_limit_bytes=32 * 2**20),
    )(here, near, far, wide, weights, place)


def column_kernel(row_ref, user_row_ref, blocks_ref, tiles_ref, out_ref):
    mine = user_row_ref[...] == row_ref[0]
    blocks = jnp.sum(jnp.where(mine, blocks_ref[...], 0), axis=1, keepdims=True)
    count = out_ref.shape[0]
    place = lax.broadcasted_iota(jnp.int32, (blocks.shape[0], count), 1) == blocks
    place = jnp.where(place, 1.0, 0.0).astype(jnp.bfloat16)
    dense = lax.dot_general(place, tiles_ref[...], (((0,), (0,)), ((), ())), preferred_element_type=f32)
    out_ref[...] = dense.astype(jnp.bfloat16)


def column_of(row, user_row, block_ids, tiles, count):
    in_vmem = pl.BlockSpec(memory_space=pltpu.VMEM)
    return pl.pallas_call(
        column_kernel,
        out_shape=jax.ShapeDtypeStruct((count, tiles.shape[1]), jnp.bfloat16),
        in_specs=[pl.BlockSpec(memory_space=pltpu.SMEM)] + [in_vmem] * 3,
    )(row.reshape(1), user_row.reshape(1, -1), block_ids.T, tiles)


def strips(user_ref, refs, fluser_ref, users_ref):
    count = fluser_ref.shape[0] // CAP
    owners = len(refs)
    for k, ref in enumerate(refs):
        fluser_ref[...] = ref[...].astype(f32)
        blocks = [fluser_ref[pl.ds(b, count, stride=CAP), :] for b in range(CAP)]
        owner = lax.rem(user_ref[0] + owners - k, owners)
        here = pl.ds(pl.multiple_of(owner * count, 16), count)
        users_ref[here, :] = jnp.concatenate(blocks, axis=1).astype(jnp.bfloat16)
    return users_ref[...]


def gram_kernel(user_ref, basis_ref, x0_ref, x1_ref, x2_ref, x3_ref, out_ref, fluser_ref, users_ref, all_ref):
    x = strips(user_ref, (x0_ref, x1_ref, x2_ref, x3_ref), fluser_ref, users_ref)
    parts = split(basis_ref[...])
    high_t, middle_t = (jnp.transpose(p.astype(f32)).astype(jnp.bfloat16) for p in parts[:2])
    one = lambda a, b: jnp.dot(a, b, preferred_element_type=f32)
    both = one(jnp.concatenate([x, high_t], axis=0), jnp.concatenate(parts, axis=1))
    strip = lambda rows, k: both[rows, RANK * k : RANK * (k + 1)]
    users, rest = slice(0, USERS), slice(USERS, None)
    small = strip(rest, 1) + strip(rest, 2)
    all_ref[:RANK, :] = strip(rest, 0) + (small + jnp.transpose(small) + one(middle_t, parts[1]))
    all_ref[RANK : 3 * RANK, :] = strip(users, 0) + (strip(users, 1) + strip(users, 2))
    cross = lax.dot_general(x, x, (((1,), (1,)), ((), ())), preferred_element_type=f32)
    all_ref[3 * RANK : 4 * RANK, :] = cross[:RANK, :RANK]
    all_ref[4 * RANK : 5 * RANK, :] = cross[:RANK, RANK:]
    all_ref[5 * RANK :, :] = cross[RANK:, RANK:]
    count, piece = out_ref.shape[:2]
    for k in range(count):
        first = (k * 4 + user_ref[0]) * piece
        out_ref[k] = all_ref[pl.ds(pl.multiple_of(first, 8), piece), :]


def gram_parts(user, basis, pieces, count):
    in_vmem = pl.BlockSpec(memory_space=pltpu.VMEM)
    return pl.pallas_call(
        gram_kernel,
        out_shape=jax.ShapeDtypeStruct((count, 6 * RANK // (count * len(pieces)), RANK), f32),
        in_specs=[pl.BlockSpec(memory_space=pltpu.SMEM)] + [in_vmem] * 5,
        scratch_shapes=[
            pltpu.VMEM(pieces[0].shape, f32),
            pltpu.VMEM((USERS, basis.shape[0]), jnp.bfloat16),
            pltpu.VMEM((6 * RANK, RANK), f32),
        ],
        compiler_params=pltpu.CompilerParams(vmem_limit_bytes=32 * 2**20),
    )(user, basis, *pieces)


def wide_kernel(
    user_ref, basis_ref, x0_ref, x1_ref, x2_ref, x3_ref, user_row_ref, weights_ref,
    out_ref, place_ref, same_ref, fluser_ref, users_ref, row_ref, sems,
):
    fetch = pltpu.make_async_copy(user_row_ref, row_ref, sems.at[0])
    hand_on = pltpu.make_async_copy(weights_ref, same_ref, sems.at[1])
    fetch.start()
    hand_on.start()
    parts = split(basis_ref[...])
    x = strips(user_ref, (x0_ref, x1_ref, x2_ref, x3_ref), fluser_ref, users_ref)
    out_ref[:, :RANK] = parts[0]
    out_ref[:, RANK:ORDER] = jnp.transpose(x.astype(f32)).astype(jnp.bfloat16)
    out_ref[:, ORDER : ORDER + RANK] = parts[1]
    out_ref[:, ORDER + RANK :] = parts[2]
    fetch.wait()
    hand_on.wait()
    user_row = row_ref[...]
    place_ref[...] = lax.rem(user_row, 4) * (user_row.shape[1] // 4) + lax.div(user_row, 4)


def wide_of(user, basis, pieces, user_row, weights):
    in_vmem, in_hbm = pl.BlockSpec(memory_space=pltpu.VMEM), pl.BlockSpec(memory_space=pltpu.HBM)
    users = user_row.shape[0]
    return pl.pallas_call(
        wide_kernel,
        out_shape=[
            jax.ShapeDtypeStruct((basis.shape[0], ORDER + 2 * RANK), jnp.bfloat16),
            jax.ShapeDtypeStruct((1, users), jnp.int32),
            jax.ShapeDtypeStruct((1, RANK), f32),
        ],
        in_specs=[pl.BlockSpec(memory_space=pltpu.SMEM)] + [in_vmem] * 5 + [in_hbm] * 2,
        out_specs=[in_vmem] * 3,
        scratch_shapes=[
            pltpu.VMEM(pieces[0].shape, f32),
            pltpu.VMEM((users, basis.shape[0]), jnp.bfloat16),
            pltpu.VMEM((1, users), jnp.int32),
            pltpu.SemaphoreType.DMA((2,)),
        ],
        compiler_params=pltpu.CompilerParams(vmem_limit_bytes=32 * 2**20),
    )(user, basis, *pieces, user_row.reshape(1, -1), weights.reshape(1, -1))


def around(x, axis):
    n = lax.axis_size(axis)
    return [lax.ppermute(x, axis, [(i, (i + k) % n) for i in range(n)]) for k in range(1, n)]


def copies(x, axes):
    x = jnp.broadcast_to(x, (lax.axis_size(axes), *x.shape))
    return lax.all_to_all(x, axes, split_axis=0, concat_axis=0, tiled=True)


def summed(parts):
    own = jnp.sum(lax.all_to_all(parts, ("item_2", "item_1"), 0, 0, tiled=True), axis=0)
    own = jnp.sum(copies(own, "item_0"), axis=0)
    half = copies(own, ("item_1", "user")).reshape(-1, RANK)
    return half, lax.ppermute(half, "item_2", [(0, 1), (1, 0)])


def per_device(basis, old_values, ratings, block_ids, user_row):
    n_item = lax.axis_size(ITEM)
    width = ratings.shape[2]
    slab_blocks = basis.shape[0] // width
    user, here = lax.axis_index("user").reshape(1), lax.axis_index("item_2").reshape(1)
    row = lax.axis_index(ITEM) * lax.axis_size("user") + lax.axis_index("user")
    column = column_of(row, user_row, block_ids, ratings[0], n_item * slab_blocks)
    arrived = lax.all_to_all(column.reshape(n_item, slab_blocks, width), ITEM, 0, 0, tiled=True)
    arrived = arrived.reshape(n_item * slab_blocks, width)
    pieces = [arrived] + around(arrived, "user")
    parts = gram_parts(user, basis, pieces, lax.axis_size("item_1") * lax.axis_size("item_2"))
    wide, place, weights = wide_of(user, basis, pieces, user_row, old_values)
    near, far = summed(parts)
    return tuple(core(here, near, far, wide, weights, place, basis.shape[0] * n_item))


def solution(mesh):
    finer = Mesh(
        mesh.devices.reshape(8, 4, 2, mesh.shape["user"]), ("item_0", "item_1", "item_2", "user")
    )
    placed = (P(ITEM, None), P(), P(ITEM_USER, None, None), P(), P())
    return jax.shard_map(
        per_device, mesh=finer, in_specs=placed, out_specs=(P(ITEM, None), P()), check_vma=False
    )
```

```python
import functools

import jax
import jax.numpy as jnp
from jax import lax
from jax.experimental import pallas as pl
from jax.experimental.pallas import tpu as pltpu
from jax.sharding import Mesh
from jax.sharding import PartitionSpec as P

ITEM = ("item_0", "item_1", "item_2")
ITEM_USER = ("item_0", "item_1", "item_2", "user")

f32 = jnp.float32
RANK, USERS, ORDER, CAP = 128, 256, 384, 4


def split(x):
    high = x.astype(jnp.bfloat16)
    rest = x - high.astype(f32)
    middle = rest.astype(jnp.bfloat16)
    return high, middle, (rest - middle.astype(f32)).astype(jnp.bfloat16)


def product(a, b, dims):
    n = a[0].shape[0]
    one = lambda x, y: lax.dot_general(x, y, (dims, ((), ())), preferred_element_type=f32)
    p = one(jnp.concatenate(a, axis=0), b[0])
    q = one(jnp.concatenate(a[:2], axis=0), b[1])
    r = one(a[0], b[2])
    return p[:n] + ((p[n : 2 * n] + q[:n]) + ((p[2 * n :] + q[n:]) + r))


def mm(a, b):
    a = a if isinstance(a, tuple) else split(a)
    b = b if isinstance(b, tuple) else split(b)
    return product(a, b, ((1,), (0,)))


def mm_nt(a, b):
    a = a if isinstance(a, tuple) else split(a)
    b = b if isinstance(b, tuple) else split(b)
    return product(a, b, ((1,), (1,)))


def spread(x):
    return jnp.broadcast_to(x, (8, RANK))


def eliminate(gram):
    lane = lax.broadcasted_iota(jnp.int32, (8, RANK), 1)
    sub = lax.broadcasted_iota(jnp.int32, (8, RANK), 0)
    count = RANK // 8
    width = 16
    deep = width // 8
    rows = [gram[8 * k : 8 * k + 8, :] for k in range(count)]
    pivots = []
    for panel in range(0, count, deep):
        first = 8 * panel
        column = [[spread(rows[panel + q][:, first + k : first + k + 1]) for k in range(width)] for q in range(deep)]
        marks = [jnp.ones((8, RANK), f32) for _ in range(deep)]
        steps = []
        for s in range(0, width, 2):
            at, r = divmod(s, 8)
            upper = [spread(column[at][k][r : r + 1, :]) for k in range(s, width)]
            under = [spread(column[at][k][r + 1 : r + 2, :]) for k in range(s + 1, width)]
            a, b, c = upper[0], upper[1], under[0]
            det = a * c - b * b
            inverse = 1.0 / a
            second = 1.0 / det
            ratio = b * inverse
            line = spread(rows[panel + at][r : r + 1, :])
            line = jnp.where(lane == first + s, line + line, line)
            next_line = spread(rows[panel + at][r + 1 : r + 2, :]) - ratio * line
            next_line = jnp.where(lane == first + s + 1, next_line + next_line, next_line)
            marks[at] = jnp.where(sub == r, a, jnp.where(sub == r + 1, det * inverse, marks[at]))
            next_inverse, mixed = a * second, b * second
            under = [x - ratio * y for x, y in zip(under, upper[1:])]
            steps.append((inverse, line, upper))
            steps.append((next_inverse, next_line, under))
            for q in range(at, deep):
                one, two = column[q][s] * inverse, column[q][s + 1] * next_inverse - column[q][s] * mixed
                if q == at:
                    one, two = jnp.where(sub > r, one, 0.0), jnp.where(sub > r + 1, two, 0.0)
                rows[panel + q] = rows[panel + q] - one * line - two * next_line
                for k in range(s + 2, width):
                    column[q][k] = column[q][k] - one * upper[k - s] - two * under[k - s - 1]
        pivots += marks
        for other in range(panel + deep, min(panel + deep + 2, count)):
            there = rows[other]
            column = [spread(there[:, first + k : first + k + 1]) for k in range(width)]
            for s, (inverse, line, upper) in enumerate(steps):
                factor = column[s] * inverse
                there = there - factor * line
                for k in range(s + 1, width):
                    column[k] = column[k] - factor * upper[k - s]
            rows[other] = there
        solved = [None] * width
        for s in range(width - 1, -1, -1):
            inverse, line, upper = steps[s]
            for k in range(s + 1, width):
                line = line - upper[k - s] * solved[k]
            solved[s] = line * inverse
        for other in range(panel + deep + 2, count):
            there = rows[other]
            for k in range(width):
                there = there - spread(rows[other][:, first + k : first + k + 1]) * solved[k]
            rows[other] = there
    return lower_of(jnp.concatenate(rows, axis=0)), jnp.concatenate(pivots, axis=0)


def square_iotas():
    i = lax.broadcasted_iota(jnp.int32, (RANK, RANK), 0)
    k = lax.broadcasted_iota(jnp.int32, (RANK, RANK), 1)
    return i, k


def lower_of(x):
    i, k = square_iotas()
    return jnp.where(i >= k, x, 0.0)


def scaled(x, pivots, power):
    factor = 1.0 / pivots if power == 1 else lax.rsqrt(pivots)
    return jnp.concatenate([x[:, c : c + RANK] * factor for c in range(0, x.shape[1], RANK)], axis=1)


def turned(lower, pivots, x):
    return scaled(mm(lower, scaled(x, pivots, 1)), pivots, 2)


def smallest(pivots, gram):
    i, k = square_iotas()
    start = jnp.sum(jnp.where(i == k, gram, 0.0), axis=1, keepdims=True)
    return jnp.min(pivots / start)


def polished(x, y):
    i, k = square_iotas()
    off = mm_nt(x, y) - jnp.where(i == k, 1.0, 0.0)
    step = jnp.where(i > k, off, jnp.where(i == k, 0.5 * off, 0.0))
    both = jnp.concatenate([x, y], axis=1)
    both = both - jnp.dot(step.astype(jnp.bfloat16), both.astype(jnp.bfloat16), preferred_element_type=f32)
    return both[:, :ORDER], both[:, ORDER:]


def assemble(sums, weights, items):
    i, k = square_iotas()
    block = lambda n: sums[RANK * n : RANK * (n + 1), :] * (1.0 / items)
    own = jnp.transpose(block(0) * weights) * weights
    left1, left2 = block(1) * weights, block(2) * weights
    c11, c12, c22 = block(3), block(4), block(5)
    diagonal = jnp.where(i == k, own + c11 + c22, 0.0)
    size = jnp.sum(diagonal, axis=(0, 1), keepdims=True)
    whole = jnp.concatenate(
        [
            jnp.concatenate([own, jnp.transpose(left1), jnp.transpose(left2)], axis=1),
            jnp.concatenate([left1, c11, c12], axis=1),
            jnp.concatenate([left2, jnp.transpose(c12), c22], axis=1),
        ],
        axis=0,
    )
    return whole * (1.0 / size), size


def core_kernel(
    items, core_ref, near_ref, far_ref, wide_ref, weights_ref, place_ref,
    rows_ref, factors_ref, sums_ref, gram_ref, turn_t_ref, back_ref,
    factored_ref, lower_ref, pivots_ref,
):
    def apart(gram):
        factored_ref[...] = gram

        @pl.when(core_ref[0] >= 0)
        def _():
            low, piv = eliminate(factored_ref[...])
            lower_ref[...] = low
            pivots_ref[...] = piv

        return lower_ref[...], pivots_ref[...]

    half = near_ref.shape[0]
    for place, ref in ((core_ref[0], near_ref), (1 - core_ref[0], far_ref)):
        sums_ref[pl.ds(pl.multiple_of(place * half, 8), half), :] = ref[...]
    weights = weights_ref[...]
    whole, size = assemble(sums_ref, weights, items)
    gram_ref[...] = whole
    g = split(whole)

    x = whole[:RANK, :]
    first = tuple(part[:RANK, :] for part in g)
    h1 = mm_nt(first, first)
    low1, piv1 = apart(h1)
    x = turned(low1, piv1, x)
    x = mm(x, g)
    part = split(x)
    h2 = mm_nt(part, part)
    low2, piv2 = apart(h2)
    x = turned(low2, piv2, x)
    x = mm(x, g)
    x = mm(x, g)
    y = mm(x, g)
    h3 = mm_nt(x, y)
    low3, piv3 = apart(h3)
    turn_t_ref[...] = turned(low3, piv3, x)
    back_ref[...] = turned(low3, piv3, y)
    fine = (smallest(piv1, h1) > 3e-5) & (smallest(piv2, h2) > 1e-4) & (smallest(piv3, h3) > 5e-5)

    @pl.when(jnp.logical_not(fine))
    def _():
        def turn(n, x):
            even = lax.rem(n, 2) == 0
            y = jnp.where(even, mm(x, split(gram_ref[...])), x)
            low, piv = eliminate(mm_nt(x, y))
            back = turned(low, piv, y)
            turn_t_ref[...] = turned(low, piv, x)
            back_ref[...] = back
            return back

        start = jnp.where(
            lax.broadcasted_iota(jnp.int32, (RANK, ORDER), 0) == lax.broadcasted_iota(jnp.int32, (RANK, ORDER), 1), 1.0, 0.0
        )
        lax.fori_loop(0, 9, turn, start)

    x, y = polished(turn_t_ref[...], back_ref[...])
    scale = lax.rsqrt(size)
    x = x * scale
    left = split(jnp.concatenate([x[:, :RANK] * weights, x[:, RANK:]], axis=1))
    one = lambda a, b: lax.dot_general(a, b, (((1,), (1,)), ((), ())), preferred_element_type=f32)
    most = one(wide_ref[:, :ORDER], jnp.concatenate(left, axis=0))
    some = one(wide_ref[:, ORDER : ORDER + RANK], jnp.concatenate([p[:, :RANK] for p in left[:2]], axis=0))
    least = one(wide_ref[:, ORDER + RANK :], left[0][:, :RANK])
    strip = lambda y, k: y[:, RANK * k : RANK * (k + 1)]
    rows_ref[...] = strip(most, 0) + ((strip(most, 1) + strip(some, 0)) + (strip(most, 2) + strip(some, 1) + least))
    taken = lax.broadcasted_iota(jnp.int32, (USERS, USERS), 0) == place_ref[...]
    taken = jnp.where(taken, 1.0, 0.0).astype(jnp.bfloat16)
    parts = jnp.concatenate(split(y[:, RANK:] * (scale * size)), axis=0)
    found = jnp.dot(parts, taken, preferred_element_type=f32)
    found = found[:RANK] + (found[RANK : 2 * RANK] + found[2 * RANK :])
    factors_ref[...] = jnp.transpose(found)


def core(here, near, far, wide, weights, place, items):
    in_vmem = pl.BlockSpec(memory_space=pltpu.VMEM)
    return pl.pallas_call(
        functools.partial(core_kernel, items),
        out_shape=[jax.ShapeDtypeStruct((wide.shape[0], RANK), f32), jax.ShapeDtypeStruct((USERS, RANK), f32)],
        in_specs=[pl.BlockSpec(memory_space=pltpu.SMEM)] + [in_vmem] * 5,
        scratch_shapes=[
            pltpu.VMEM((2 * ORDER, RANK), f32),
            pltpu.VMEM((ORDER, ORDER), f32),
            pltpu.VMEM((RANK, ORDER), f32),
            pltpu.VMEM((RANK, ORDER), f32),
        ]
        + [pltpu.VMEM((RANK, RANK), f32)] * 3,
        compiler_params=pltpu.CompilerParams(vmem_limit_bytes=32 * 2**20),
    )(here, near, far, wide, weights, place)


def column_kernel(row_ref, user_row_ref, blocks_ref, tiles_ref, out_ref):
    mine = user_row_ref[...] == row_ref[0]
    blocks = jnp.sum(jnp.where(mine, blocks_ref[...], 0), axis=1, keepdims=True)
    count = out_ref.shape[0]
    place = lax.broadcasted_iota(jnp.int32, (blocks.shape[0], count), 1) == blocks
    place = jnp.where(place, 1.0, 0.0).astype(jnp.bfloat16)
    dense = lax.dot_general(place, tiles_ref[...], (((0,), (0,)), ((), ())), preferred_element_type=f32)
    out_ref[...] = dense.astype(jnp.bfloat16)


def column_of(row, user_row, block_ids, tiles, count):
    in_vmem = pl.BlockSpec(memory_space=pltpu.VMEM)
    return pl.pallas_call(
        column_kernel,
        out_shape=jax.ShapeDtypeStruct((count, tiles.shape[1]), jnp.bfloat16),
        in_specs=[pl.BlockSpec(memory_space=pltpu.SMEM)] + [in_vmem] * 3,
    )(row.reshape(1), user_row.reshape(1, -1), block_ids.T, tiles)


def strips(user_ref, refs, fluser_ref, users_ref):
    count = fluser_ref.shape[0] // CAP
    owners = len(refs)
    for k, ref in enumerate(refs):
        fluser_ref[...] = ref[...].astype(f32)
        blocks = [fluser_ref[pl.ds(b, count, stride=CAP), :] for b in range(CAP)]
        owner = lax.rem(user_ref[0] + owners - k, owners)
        here = pl.ds(pl.multiple_of(owner * count, 16), count)
        users_ref[here, :] = jnp.concatenate(blocks, axis=1).astype(jnp.bfloat16)
    return users_ref[...]


def gram_kernel(user_ref, basis_ref, x0_ref, x1_ref, x2_ref, x3_ref, out_ref, fluser_ref, users_ref, all_ref):
    x = strips(user_ref, (x0_ref, x1_ref, x2_ref, x3_ref), fluser_ref, users_ref)
    parts = split(basis_ref[...])
    high_t, middle_t = (jnp.transpose(p.astype(f32)).astype(jnp.bfloat16) for p in parts[:2])
    one = lambda a, b: jnp.dot(a, b, preferred_element_type=f32)
    both = one(jnp.concatenate([x, high_t], axis=0), jnp.concatenate(parts, axis=1))
    strip = lambda rows, k: both[rows, RANK * k : RANK * (k + 1)]
    users, rest = slice(0, USERS), slice(USERS, None)
    small = strip(rest, 1) + strip(rest, 2)
    all_ref[:RANK, :] = strip(rest, 0) + (small + jnp.transpose(small) + one(middle_t, parts[1]))
    all_ref[RANK : 3 * RANK, :] = strip(users, 0) + (strip(users, 1) + strip(users, 2))
    cross = lax.dot_general(x, x, (((1,), (1,)), ((), ())), preferred_element_type=f32)
    all_ref[3 * RANK : 4 * RANK, :] = cross[:RANK, :RANK]
    all_ref[4 * RANK : 5 * RANK, :] = cross[:RANK, RANK:]
    all_ref[5 * RANK :, :] = cross[RANK:, RANK:]
    count, piece = out_ref.shape[:2]
    for k in range(count):
        first = (k * 4 + user_ref[0]) * piece
        out_ref[k] = all_ref[pl.ds(pl.multiple_of(first, 8), piece), :]


def gram_parts(user, basis, pieces, count):
    in_vmem = pl.BlockSpec(memory_space=pltpu.VMEM)
    return pl.pallas_call(
        gram_kernel,
        out_shape=jax.ShapeDtypeStruct((count, 6 * RANK // (count * len(pieces)), RANK), f32),
        in_specs=[pl.BlockSpec(memory_space=pltpu.SMEM)] + [in_vmem] * 5,
        scratch_shapes=[
            pltpu.VMEM(pieces[0].shape, f32),
            pltpu.VMEM((USERS, basis.shape[0]), jnp.bfloat16),
            pltpu.VMEM((6 * RANK, RANK), f32),
        ],
        compiler_params=pltpu.CompilerParams(vmem_limit_bytes=32 * 2**20),
    )(user, basis, *pieces)


def wide_kernel(
    user_ref, basis_ref, x0_ref, x1_ref, x2_ref, x3_ref, user_row_ref, weights_ref,
    out_ref, place_ref, same_ref, fluser_ref, users_ref, row_ref, sems,
):
    fetch = pltpu.make_async_copy(user_row_ref, row_ref, sems.at[0])
    hand_on = pltpu.make_async_copy(weights_ref, same_ref, sems.at[1])
    fetch.start()
    hand_on.start()
    parts = split(basis_ref[...])
    x = strips(user_ref, (x0_ref, x1_ref, x2_ref, x3_ref), fluser_ref, users_ref)
    out_ref[:, :RANK] = parts[0]
    out_ref[:, RANK:ORDER] = jnp.transpose(x.astype(f32)).astype(jnp.bfloat16)
    out_ref[:, ORDER : ORDER + RANK] = parts[1]
    out_ref[:, ORDER + RANK :] = parts[2]
    fetch.wait()
    hand_on.wait()
    user_row = row_ref[...]
    place_ref[...] = lax.rem(user_row, 4) * (user_row.shape[1] // 4) + lax.div(user_row, 4)


def wide_of(user, basis, pieces, user_row, weights):
    in_vmem, in_hbm = pl.BlockSpec(memory_space=pltpu.VMEM), pl.BlockSpec(memory_space=pltpu.HBM)
    users = user_row.shape[0]
    return pl.pallas_call(
        wide_kernel,
        out_shape=[
            jax.ShapeDtypeStruct((basis.shape[0], ORDER + 2 * RANK), jnp.bfloat16),
            jax.ShapeDtypeStruct((1, users), jnp.int32),
            jax.ShapeDtypeStruct((1, RANK), f32),
        ],
        in_specs=[pl.BlockSpec(memory_space=pltpu.SMEM)] + [in_vmem] * 5 + [in_hbm] * 2,
        out_specs=[in_vmem] * 3,
        scratch_shapes=[
            pltpu.VMEM(pieces[0].shape, f32),
            pltpu.VMEM((users, basis.shape[0]), jnp.bfloat16),
            pltpu.VMEM((1, users), jnp.int32),
            pltpu.SemaphoreType.DMA((2,)),
        ],
        compiler_params=pltpu.CompilerParams(vmem_limit_bytes=32 * 2**20),
    )(user, basis, *pieces, user_row.reshape(1, -1), weights.reshape(1, -1))


def around(x, axis):
    n = lax.axis_size(axis)
    return [lax.ppermute(x, axis, [(i, (i + k) % n) for i in range(n)]) for k in range(1, n)]


def copies(x, axes):
    x = jnp.broadcast_to(x, (lax.axis_size(axes), *x.shape))
    return lax.all_to_all(x, axes, split_axis=0, concat_axis=0, tiled=True)


def summed(parts):
    own = jnp.sum(lax.all_to_all(parts, ("item_2", "item_1"), 0, 0, tiled=True), axis=0)
    own = jnp.sum(copies(own, "item_0"), axis=0)
    half = copies(own, ("item_1", "user")).reshape(-1, RANK)
    return half, lax.ppermute(half, "item_2", [(0, 1), (1, 0)])


def per_device(basis, old_values, ratings, block_ids, user_row):
    n_item = lax.axis_size(ITEM)
    width = ratings.shape[2]
    slab_blocks = basis.shape[0] // width
    user, here = lax.axis_index("user").reshape(1), lax.axis_index("item_2").reshape(1)
    row = lax.axis_index(ITEM) * lax.axis_size("user") + lax.axis_index("user")
    column = column_of(row, user_row, block_ids, ratings[0], n_item * slab_blocks)
    arrived = lax.all_to_all(column.reshape(n_item, slab_blocks, width), ITEM, 0, 0, tiled=True)
    arrived = arrived.reshape(n_item * slab_blocks, width)
    pieces = [arrived] + around(arrived, "user")
    parts = gram_parts(user, basis, pieces, lax.axis_size("item_1") * lax.axis_size("item_2"))
    wide, place, weights = wide_of(user, basis, pieces, user_row, old_values)
    near, far = summed(parts)
    return tuple(core(here, near, far, wide, weights, place, basis.shape[0] * n_item))


def solution(mesh):
    finer = Mesh(
        mesh.devices.reshape(8, 4, 2, mesh.shape["user"]), ("item_0", "item_1", "item_2", "user")
    )
    placed = (P(ITEM, None), P(), P(ITEM_USER, None, None), P(), P())
    return jax.shard_map(
        per_device, mesh=finer, in_specs=placed, out_specs=(P(ITEM, None), P()), check_vma=False
    )
```

```python
import functools

import jax
import jax.numpy as jnp
from jax import lax
from jax.experimental import pallas as pl
from jax.experimental.pallas import tpu as pltpu
from jax.sharding import Mesh
from jax.sharding import PartitionSpec as P

ITEM = ("item_0", "item_1", "item_2")
ITEM_USER = ("item_0", "item_1", "item_2", "user")

f32 = jnp.float32
RANK, USERS, ORDER, CAP = 128, 256, 384, 4


def split(x):
    high = x.astype(jnp.bfloat16)
    rest = x - high.astype(f32)
    middle = rest.astype(jnp.bfloat16)
    return high, middle, (rest - middle.astype(f32)).astype(jnp.bfloat16)


def product(a, b, dims):
    n = a[0].shape[0]
    one = lambda x, y: lax.dot_general(x, y, (dims, ((), ())), preferred_element_type=f32)
    p = one(jnp.concatenate(a, axis=0), b[0])
    q = one(jnp.concatenate(a[:2], axis=0), b[1])
    r = one(a[0], b[2])
    return p[:n] + ((p[n : 2 * n] + q[:n]) + ((p[2 * n :] + q[n:]) + r))


def mm(a, b):
    a = a if isinstance(a, tuple) else split(a)
    b = b if isinstance(b, tuple) else split(b)
    return product(a, b, ((1,), (0,)))


def mm_nt(a, b):
    a = a if isinstance(a, tuple) else split(a)
    b = b if isinstance(b, tuple) else split(b)
    return product(a, b, ((1,), (1,)))


def spread(x):
    return jnp.broadcast_to(x, (8, RANK))


def eliminate(gram):
    lane = lax.broadcasted_iota(jnp.int32, (8, RANK), 1)
    sub = lax.broadcasted_iota(jnp.int32, (8, RANK), 0)
    count = RANK // 8
    width = 16
    deep = width // 8
    rows = [gram[8 * k : 8 * k + 8, :] for k in range(count)]
    pivots = []
    for panel in range(0, count, deep):
        first = 8 * panel
        column = [[spread(rows[panel + q][:, first + k : first + k + 1]) for k in range(width)] for q in range(deep)]
        marks = [jnp.ones((8, RANK), f32) for _ in range(deep)]
        steps = []
        for s in range(0, width, 2):
            at, r = divmod(s, 8)
            upper = [spread(column[at][k][r : r + 1, :]) for k in range(s, width)]
            under = [spread(column[at][k][r + 1 : r + 2, :]) for k in range(s + 1, width)]
            a, b, c = upper[0], upper[1], under[0]
            det = a * c - b * b
            inverse = 1.0 / a
            second = 1.0 / det
            ratio = b * inverse
            line = spread(rows[panel + at][r : r + 1, :])
            line = jnp.where(lane == first + s, line + line, line)
            next_line = spread(rows[panel + at][r + 1 : r + 2, :]) - ratio * line
            next_line = jnp.where(lane == first + s + 1, next_line + next_line, next_line)
            marks[at] = jnp.where(sub == r, a, jnp.where(sub == r + 1, det * inverse, marks[at]))
            next_inverse, mixed = a * second, b * second
            under = [x - ratio * y for x, y in zip(under, upper[1:])]
            steps.append((inverse, line, upper))
            steps.append((next_inverse, next_line, under))
            for q in range(at, deep):
                one, two = column[q][s] * inverse, column[q][s + 1] * next_inverse - column[q][s] * mixed
                if q == at:
                    one, two = jnp.where(sub > r, one, 0.0), jnp.where(sub > r + 1, two, 0.0)
                rows[panel + q] = rows[panel + q] - one * line - two * next_line
                for k in range(s + 2, width):
                    column[q][k] = column[q][k] - one * upper[k - s] - two * under[k - s - 1]
        pivots += marks
        for other in range(panel + deep, min(panel + deep + 2, count)):
            there = rows[other]
            column = [spread(there[:, first + k : first + k + 1]) for k in range(width)]
            for s, (inverse, line, upper) in enumerate(steps):
                factor = column[s] * inverse
                there = there - factor * line
                for k in range(s + 1, width):
                    column[k] = column[k] - factor * upper[k - s]
            rows[other] = there
        solved = [None] * width
        for s in range(width - 1, -1, -1):
            inverse, line, upper = steps[s]
            for k in range(s + 1, width):
                line = line - upper[k - s] * solved[k]
            solved[s] = line * inverse
        for other in range(panel + deep + 2, count):
            there = rows[other]
            for k in range(width):
                there = there - spread(rows[other][:, first + k : first + k + 1]) * solved[k]
            rows[other] = there
    return lower_of(jnp.concatenate(rows, axis=0)), jnp.concatenate(pivots, axis=0)


def square_iotas():
    i = lax.broadcasted_iota(jnp.int32, (RANK, RANK), 0)
    k = lax.broadcasted_iota(jnp.int32, (RANK, RANK), 1)
    return i, k


def lower_of(x):
    i, k = square_iotas()
    return jnp.where(i >= k, x, 0.0)


def scaled(x, pivots, power):
    factor = 1.0 / pivots if power == 1 else lax.rsqrt(pivots)
    return jnp.concatenate([x[:, c : c + RANK] * factor for c in range(0, x.shape[1], RANK)], axis=1)


def turned(lower, pivots, x):
    return scaled(mm(lower, scaled(x, pivots, 1)), pivots, 2)


def smallest(pivots, gram):
    i, k = square_iotas()
    start = jnp.sum(jnp.where(i == k, gram, 0.0), axis=1, keepdims=True)
    ratio = pivots / start
    return jnp.min(jnp.where((ratio > 0.0) & (ratio < 2.0), ratio, 0.0))


def polished(x, y):
    i, k = square_iotas()
    off = mm_nt(x, y) - jnp.where(i == k, 1.0, 0.0)
    step = jnp.where(i > k, off, jnp.where(i == k, 0.5 * off, 0.0))
    both = jnp.concatenate([x, y], axis=1)
    both = both - jnp.dot(step.astype(jnp.bfloat16), both.astype(jnp.bfloat16), preferred_element_type=f32)
    return both[:, :ORDER], both[:, ORDER:]


def assemble(sums, weights, items):
    i, k = square_iotas()
    block = lambda n: sums[RANK * n : RANK * (n + 1), :] * (1.0 / items)
    own = jnp.transpose(block(0) * weights) * weights
    left1, left2 = block(1) * weights, block(2) * weights
    c11, c12, c22 = block(3), block(4), block(5)
    diagonal = jnp.where(i == k, own + c11 + c22, 0.0)
    size = jnp.sum(diagonal, axis=(0, 1), keepdims=True)
    whole = jnp.concatenate(
        [
            jnp.concatenate([own, jnp.transpose(left1), jnp.transpose(left2)], axis=1),
            jnp.concatenate([left1, c11, c12], axis=1),
            jnp.concatenate([left2, jnp.transpose(c12), c22], axis=1),
        ],
        axis=0,
    )
    return whole * (1.0 / size), size


def core_kernel(
    items, core_ref, near_ref, far_ref, wide_ref, weights_ref, place_ref,
    rows_ref, factors_ref, sums_ref, gram_ref, turn_t_ref, back_ref,
    factored_ref, lower_ref, pivots_ref,
):
    def apart(gram):
        factored_ref[...] = gram

        @pl.when(core_ref[0] >= 0)
        def _():
            low, piv = eliminate(factored_ref[...])
            lower_ref[...] = low
            pivots_ref[...] = piv

        return lower_ref[...], pivots_ref[...]

    half = near_ref.shape[0]
    for place, ref in ((core_ref[0], near_ref), (1 - core_ref[0], far_ref)):
        sums_ref[pl.ds(pl.multiple_of(place * half, 8), half), :] = ref[...]
    weights = weights_ref[...]
    whole, size = assemble(sums_ref, weights, items)
    gram_ref[...] = whole
    g = split(whole)

    x = whole[:RANK, :]
    first = tuple(part[:RANK, :] for part in g)
    h1 = mm_nt(first, first)
    low1, piv1 = apart(h1)
    x = turned(low1, piv1, x)
    x = mm(x, g)
    part = split(x)
    h2 = mm_nt(part, part)
    low2, piv2 = apart(h2)
    x = turned(low2, piv2, x)
    x = mm(x, g)
    x = mm(x, g)
    y = mm(x, g)
    h3 = mm_nt(x, y)
    low3, piv3 = apart(h3)
    turn_t_ref[...] = turned(low3, piv3, x)
    back_ref[...] = turned(low3, piv3, y)
    fine = (smallest(piv1, h1) > 3e-5) & (smallest(piv2, h2) > 1e-4) & (smallest(piv3, h3) > 5e-5)

    @pl.when(jnp.logical_not(fine))
    def _():
        def turn(n, x):
            even = lax.rem(n, 2) == 0
            y = jnp.where(even, mm(x, split(gram_ref[...])), x)
            low, piv = eliminate(mm_nt(x, y))
            back = turned(low, piv, y)
            turn_t_ref[...] = turned(low, piv, x)
            back_ref[...] = back
            return back

        start = jnp.where(
            lax.broadcasted_iota(jnp.int32, (RANK, ORDER), 0) == lax.broadcasted_iota(jnp.int32, (RANK, ORDER), 1), 1.0, 0.0
        )
        lax.fori_loop(0, 9, turn, start)

    x, y = polished(turn_t_ref[...], back_ref[...])
    scale = lax.rsqrt(size)
    x = x * scale
    left = split(jnp.concatenate([x[:, :RANK] * weights, x[:, RANK:]], axis=1))
    one = lambda a, b: lax.dot_general(a, b, (((1,), (1,)), ((), ())), preferred_element_type=f32)
    most = one(wide_ref[:, :ORDER], jnp.concatenate(left, axis=0))
    some = one(wide_ref[:, ORDER : ORDER + RANK], jnp.concatenate([p[:, :RANK] for p in left[:2]], axis=0))
    least = one(wide_ref[:, ORDER + RANK :], left[0][:, :RANK])
    strip = lambda y, k: y[:, RANK * k : RANK * (k + 1)]
    rows_ref[...] = strip(most, 0) + ((strip(most, 1) + strip(some, 0)) + (strip(most, 2) + strip(some, 1) + least))
    taken = lax.broadcasted_iota(jnp.int32, (USERS, USERS), 0) == place_ref[...]
    taken = jnp.where(taken, 1.0, 0.0).astype(jnp.bfloat16)
    parts = jnp.concatenate(split(y[:, RANK:] * (scale * size)), axis=0)
    found = jnp.dot(parts, taken, preferred_element_type=f32)
    found = found[:RANK] + (found[RANK : 2 * RANK] + found[2 * RANK :])
    factors_ref[...] = jnp.transpose(found)


def core(here, near, far, wide, weights, place, items):
    in_vmem = pl.BlockSpec(memory_space=pltpu.VMEM)
    return pl.pallas_call(
        functools.partial(core_kernel, items),
        out_shape=[jax.ShapeDtypeStruct((wide.shape[0], RANK), f32), jax.ShapeDtypeStruct((USERS, RANK), f32)],
        in_specs=[pl.BlockSpec(memory_space=pltpu.SMEM)] + [in_vmem] * 5,
        scratch_shapes=[
            pltpu.VMEM((2 * ORDER, RANK), f32),
            pltpu.VMEM((ORDER, ORDER), f32),
            pltpu.VMEM((RANK, ORDER), f32),
            pltpu.VMEM((RANK, ORDER), f32),
        ]
        + [pltpu.VMEM((RANK, RANK), f32)] * 3,
        compiler_params=pltpu.CompilerParams(vmem_limit_bytes=32 * 2**20),
    )(here, near, far, wide, weights, place)


def column_kernel(row_ref, user_row_ref, blocks_ref, tiles_ref, out_ref):
    mine = user_row_ref[...] == row_ref[0]
    blocks = jnp.sum(jnp.where(mine, blocks_ref[...], 0), axis=1, keepdims=True)
    count = out_ref.shape[0]
    place = lax.broadcasted_iota(jnp.int32, (blocks.shape[0], count), 1) == blocks
    place = jnp.where(place, 1.0, 0.0).astype(jnp.bfloat16)
    dense = lax.dot_general(place, tiles_ref[...], (((0,), (0,)), ((), ())), preferred_element_type=f32)
    out_ref[...] = dense.astype(jnp.bfloat16)


def column_of(row, user_row, block_ids, tiles, count):
    in_vmem = pl.BlockSpec(memory_space=pltpu.VMEM)
    return pl.pallas_call(
        column_kernel,
        out_shape=jax.ShapeDtypeStruct((count, tiles.shape[1]), jnp.bfloat16),
        in_specs=[pl.BlockSpec(memory_space=pltpu.SMEM)] + [in_vmem] * 3,
    )(row.reshape(1), user_row.reshape(1, -1), block_ids.T, tiles)


def strips(user_ref, refs, fluser_ref, users_ref):
    count = fluser_ref.shape[0] // CAP
    owners = len(refs)
    for k, ref in enumerate(refs):
        fluser_ref[...] = ref[...].astype(f32)
        blocks = [fluser_ref[pl.ds(b, count, stride=CAP), :] for b in range(CAP)]
        owner = lax.rem(user_ref[0] + owners - k, owners)
        here = pl.ds(pl.multiple_of(owner * count, 16), count)
        users_ref[here, :] = jnp.concatenate(blocks, axis=1).astype(jnp.bfloat16)
    return users_ref[...]


def gram_kernel(user_ref, basis_ref, x0_ref, x1_ref, x2_ref, x3_ref, out_ref, fluser_ref, users_ref, all_ref):
    x = strips(user_ref, (x0_ref, x1_ref, x2_ref, x3_ref), fluser_ref, users_ref)
    parts = split(basis_ref[...])
    high_t, middle_t = (jnp.transpose(p.astype(f32)).astype(jnp.bfloat16) for p in parts[:2])
    one = lambda a, b: jnp.dot(a, b, preferred_element_type=f32)
    both = one(jnp.concatenate([x, high_t], axis=0), jnp.concatenate(parts, axis=1))
    strip = lambda rows, k: both[rows, RANK * k : RANK * (k + 1)]
    users, rest = slice(0, USERS), slice(USERS, None)
    small = strip(rest, 1) + strip(rest, 2)
    all_ref[:RANK, :] = strip(rest, 0) + (small + jnp.transpose(small) + one(middle_t, parts[1]))
    all_ref[RANK : 3 * RANK, :] = strip(users, 0) + (strip(users, 1) + strip(users, 2))
    cross = lax.dot_general(x, x, (((1,), (1,)), ((), ())), preferred_element_type=f32)
    all_ref[3 * RANK : 4 * RANK, :] = cross[:RANK, :RANK]
    all_ref[4 * RANK : 5 * RANK, :] = cross[:RANK, RANK:]
    all_ref[5 * RANK :, :] = cross[RANK:, RANK:]
    count, piece = out_ref.shape[:2]
    for k in range(count):
        first = (k * 4 + user_ref[0]) * piece
        out_ref[k] = all_ref[pl.ds(pl.multiple_of(first, 8), piece), :]


def gram_parts(user, basis, pieces, count):
    in_vmem = pl.BlockSpec(memory_space=pltpu.VMEM)
    return pl.pallas_call(
        gram_kernel,
        out_shape=jax.ShapeDtypeStruct((count, 6 * RANK // (count * len(pieces)), RANK), f32),
        in_specs=[pl.BlockSpec(memory_space=pltpu.SMEM)] + [in_vmem] * 5,
        scratch_shapes=[
            pltpu.VMEM(pieces[0].shape, f32),
            pltpu.VMEM((USERS, basis.shape[0]), jnp.bfloat16),
            pltpu.VMEM((6 * RANK, RANK), f32),
        ],
        compiler_params=pltpu.CompilerParams(vmem_limit_bytes=32 * 2**20),
    )(user, basis, *pieces)


def wide_kernel(
    user_ref, basis_ref, x0_ref, x1_ref, x2_ref, x3_ref, user_row_ref, weights_ref,
    out_ref, place_ref, same_ref, fluser_ref, users_ref, row_ref, sems,
):
    fetch = pltpu.make_async_copy(user_row_ref, row_ref, sems.at[0])
    hand_on = pltpu.make_async_copy(weights_ref, same_ref, sems.at[1])
    fetch.start()
    hand_on.start()
    parts = split(basis_ref[...])
    x = strips(user_ref, (x0_ref, x1_ref, x2_ref, x3_ref), fluser_ref, users_ref)
    out_ref[:, :RANK] = parts[0]
    out_ref[:, RANK:ORDER] = jnp.transpose(x.astype(f32)).astype(jnp.bfloat16)
    out_ref[:, ORDER : ORDER + RANK] = parts[1]
    out_ref[:, ORDER + RANK :] = parts[2]
    fetch.wait()
    hand_on.wait()
    user_row = row_ref[...]
    place_ref[...] = lax.rem(user_row, 4) * (user_row.shape[1] // 4) + lax.div(user_row, 4)


def wide_of(user, basis, pieces, user_row, weights):
    in_vmem, in_hbm = pl.BlockSpec(memory_space=pltpu.VMEM), pl.BlockSpec(memory_space=pltpu.HBM)
    users = user_row.shape[0]
    return pl.pallas_call(
        wide_kernel,
        out_shape=[
            jax.ShapeDtypeStruct((basis.shape[0], ORDER + 2 * RANK), jnp.bfloat16),
            jax.ShapeDtypeStruct((1, users), jnp.int32),
            jax.ShapeDtypeStruct((1, RANK), f32),
        ],
        in_specs=[pl.BlockSpec(memory_space=pltpu.SMEM)] + [in_vmem] * 5 + [in_hbm] * 2,
        out_specs=[in_vmem] * 3,
        scratch_shapes=[
            pltpu.VMEM(pieces[0].shape, f32),
            pltpu.VMEM((users, basis.shape[0]), jnp.bfloat16),
            pltpu.VMEM((1, users), jnp.int32),
            pltpu.SemaphoreType.DMA((2,)),
        ],
        compiler_params=pltpu.CompilerParams(vmem_limit_bytes=32 * 2**20),
    )(user, basis, *pieces, user_row.reshape(1, -1), weights.reshape(1, -1))


def around(x, axis):
    n = lax.axis_size(axis)
    return [lax.ppermute(x, axis, [(i, (i + k) % n) for i in range(n)]) for k in range(1, n)]


def copies(x, axes):
    x = jnp.broadcast_to(x, (lax.axis_size(axes), *x.shape))
    return lax.all_to_all(x, axes, split_axis=0, concat_axis=0, tiled=True)


def summed(parts):
    own = jnp.sum(lax.all_to_all(parts, ("item_2", "item_1"), 0, 0, tiled=True), axis=0)
    own = jnp.sum(copies(own, "item_0"), axis=0)
    half = copies(own, ("item_1", "user")).reshape(-1, RANK)
    return half, lax.ppermute(half, "item_2", [(0, 1), (1, 0)])


def per_device(basis, old_values, ratings, block_ids, user_row):
    n_item = lax.axis_size(ITEM)
    width = ratings.shape[2]
    slab_blocks = basis.shape[0] // width
    user, here = lax.axis_index("user").reshape(1), lax.axis_index("item_2").reshape(1)
    row = lax.axis_index(ITEM) * lax.axis_size("user") + lax.axis_index("user")
    column = column_of(row, user_row, block_ids, ratings[0], n_item * slab_blocks)
    arrived = lax.all_to_all(column.reshape(n_item, slab_blocks, width), ITEM, 0, 0, tiled=True)
    arrived = arrived.reshape(n_item * slab_blocks, width)
    pieces = [arrived] + around(arrived, "user")
    parts = gram_parts(user, basis, pieces, lax.axis_size("item_1") * lax.axis_size("item_2"))
    wide, place, weights = wide_of(user, basis, pieces, user_row, old_values)
    near, far = summed(parts)
    return tuple(core(here, near, far, wide, weights, place, basis.shape[0] * n_item))


def solution(mesh):
    finer = Mesh(
        mesh.devices.reshape(8, 4, 2, mesh.shape["user"]), ("item_0", "item_1", "item_2", "user")
    )
    placed = (P(ITEM, None), P(), P(ITEM_USER, None, None), P(), P())
    return jax.shard_map(
        per_device, mesh=finer, in_specs=placed, out_specs=(P(ITEM, None), P()), check_vma=False
    )
```
